512 devices in a mesh: blk: 128 (over z, x_hi, y), grp: 4 (over x_lo, core).
Axes of the slice: x: 4 (x_hi: 2, x_lo: 2; x = x_hi * 2 + x_lo), y: 8, z: 8, core: 2. Of those that a mesh axis runs over, the one named last changes fastest.
Arguments:
- feats: bfloat16 [131072, 1152], P(('blk', 'grp')), may hold values from -6 to 6
- proj_weight: bfloat16 [1152, 1152], P('grp'), may hold values from -0.1875 to 0.1875
- text_embed: bfloat16 [131072, 1152], P(('blk', 'grp')), may hold values from -6 to 6
- row_ids: int32 [131072], P(('blk', 'grp')), may hold values from 0 to 127
- logit_scale: float32 [1], replicated, may hold values from 2 to 10
- logit_bias: float32 [1], replicated, may hold values from -4 to -1
Outputs:
- weight_grad: float32 [1152, 1152], P('grp')
- text_grad: float32 [131072, 1152], P(('blk', 'grp'))
The draws below stay inside these ranges and needn't reach their ends.
All inputs are finite; a program needn't handle non-finite values.
Results may differ from the reference program's by a relative error of at most 0.014.
Values may be sent and summed in bfloat16 or wider, within the bound.
No kernel may reach another device: no remote copies, remote signals or barrier semaphores. Data moves between devices by JAX's collectives and lax.ppermute only.
A program may use at most 64 MiB of HBM per device.

```python
import math
import jax
import jax.numpy as jnp
from jax import lax

D = 1152
TOK_DEV = 256
STEPS = 4
IDS = 128
TOKENS = 131072
N_BLK = 128
N_GRP = 4


def with_ends(result, own_key, smallest, largest):
    index_at = [jax.random.randint(jax.random.fold_in(own_key, axis), (), 0, length) for axis, length in enumerate(result.shape)]
    longest = result.shape.index(max(result.shape))
    next_to = index_at[:longest] + [(index_at[longest] + 1) % result.shape[longest]] + index_at[longest + 1:]
    return result.at[tuple(index_at)].set(smallest).at[tuple(next_to)].set(largest)


def levels(rng, dims, cuts, least, high):
    factor_of, own = 1.0, jax.random.fold_in(rng, 6)
    for axis_at, blocks in cuts:
        heights = jnp.exp(jax.random.uniform(jax.random.fold_in(own, axis_at), (blocks,), jnp.float32, least / len(cuts), high / len(cuts)))
        factor_of = factor_of * jnp.repeat(heights, dims[axis_at] // blocks).reshape([-1 if axis == axis_at else 1 for axis in range(len(dims))])
    return factor_of


def scatter_about(stream_key, shape, scale, limit, cuts=(), kind=jnp.bfloat16):
    drawn = jax.random.normal(stream_key, shape, jnp.float32) * scale
    if len(cuts) > 0:
        drawn = levels(stream_key, shape, cuts, -0.22, 0.18) * drawn
    return jnp.clip(drawn, min=-limit, max=limit).astype(kind)


def setup_inputs(seed: int = 0) -> dict:
    key_of = jax.random.split(jax.random.key(seed), 7)
    return {
        "feats": scatter_about(key_of[0], (TOKENS, D), 1.0, 6.0, ((0, 512),)),
        "proj_weight": scatter_about(key_of[1], (D, D), D ** -0.5, 0.1875, ((0, 4),)),
        "text_embed": scatter_about(key_of[2], (TOKENS, D), 1.0, 6.0, ((0, 512),)),
        "row_ids": with_ends(jax.random.randint(key_of[3], (TOKENS,), 0, IDS), jax.random.fold_in(key_of[3], 1), 0, IDS - 1).astype(jnp.int32),
        "logit_scale": jnp.clip(jnp.exp(jax.random.uniform(key_of[4], (1,), jnp.float32, math.log(2.0), math.log(10.0))), 2.0, 10.0),
        "logit_bias": jnp.clip(jax.random.uniform(key_of[5], (1,), jnp.float32, -4.0, -1.0), -4.0, -1.0),
    }


def reference(feats, proj_weight, text_embed, row_ids, logit_scale, logit_bias):
    scale = logit_scale[0]
    bias = logit_bias[0]
    raw = jnp.dot(feats, proj_weight, preferred_element_type=jnp.float32)
    radius = jnp.sqrt(lax.optimization_barrier(jnp.sum(raw * raw, -1, keepdims=True)) + 1e-06)
    unit = raw / radius
    image_unit = unit.astype(jnp.bfloat16)
    text_f = text_embed.astype(jnp.float32)
    text_unit = (text_f / jnp.sqrt(lax.optimization_barrier(jnp.sum(text_f * text_f, -1, keepdims=True)) + 1e-06)).astype(jnp.bfloat16)
    nblk = N_BLK
    ngrp = N_GRP
    image_four = image_unit.astype(jnp.float32).reshape(nblk, ngrp, TOK_DEV, D)
    text_four = text_unit.astype(jnp.float32).reshape(nblk, ngrp, TOK_DEV, D)
    ids_four = row_ids.reshape(nblk, ngrp, TOK_DEV)
    image_grad = jnp.zeros((nblk, ngrp, TOK_DEV, D), jnp.float32)
    text_grad = jnp.zeros((nblk, ngrp, TOK_DEV, D), jnp.float32)
    for step in range(STEPS):
        met = jnp.roll(text_four, step, axis=0)
        met_ids = jnp.roll(ids_four, step, axis=0)
        logits = scale * jnp.einsum('bgid,bgjd->bgij', image_four, met) + bias
        sign = jnp.where(ids_four[:, :, :, None] == met_ids[:, :, None, :], 1.0, -1.0).astype(jnp.float32)
        pair_weight = (-sign * jax.nn.sigmoid(-sign * logits)).astype(jnp.bfloat16).astype(jnp.float32)
        image_grad = image_grad + scale * jnp.einsum('bgij,bgjd->bgid', pair_weight, met)
        text_part = scale * jnp.einsum('bgij,bgid->bgjd', pair_weight, image_four)
        text_grad = text_grad + jnp.roll(text_part, -step, axis=0)
    image_grad = image_grad.reshape(-1, D)
    text_grad = text_grad.reshape(-1, D)
    inner = lax.optimization_barrier(jnp.sum(image_grad * unit, -1, keepdims=True))
    raw_grad = ((image_grad - unit * inner) / radius).astype(jnp.bfloat16)
    feats_four = feats.reshape(nblk, ngrp, TOK_DEV, D)
    grad_four = raw_grad.reshape(nblk, ngrp, TOK_DEV, D)

    def accumulate(total, pieces):
        feat_blk, grad_blk = pieces
        parts = jnp.einsum('gri,grj->gij', feat_blk.astype(jnp.float32), grad_blk.astype(jnp.float32))
        parts = parts.astype(jnp.bfloat16).astype(jnp.float32)
        return (total + lax.optimization_barrier(jnp.sum(parts, 0)), None)
    weight_grad, unused = lax.scan(accumulate, jnp.zeros((D, D), jnp.float32), (feats_four, grad_four))
    return (weight_grad, text_grad)
```

```python
import jax
import jax.numpy as jnp
from jax import lax
from jax.sharding import Mesh, PartitionSpec as P

BF = jnp.bfloat16
F32 = jnp.float32
ROWS = 256
D = 1152
SHARD = D // 4
SUB = SHARD // 4
SPLIT = ("z2", "z1", "z0", "xh", "y2", "y1", "y0", "xl", "core")
BLK = SPLIT[:7]
NEAR = ("z0", "y0")
FAR = ("z2", "z1", "xh", "y2", "y1")


def shift(block, distance):
    n = 128
    return lax.ppermute(block, BLK, [((i - distance) % n, i) for i in range(n)])


def swap(block, axis):
    return lax.ppermute(block, axis, [(0, 1), (1, 0)])


def exchange(chunks, axes):
    return lax.all_to_all(chunks, axes, 0, 0, tiled=True)


def spread(chunk, axes, n):
    return exchange(jnp.broadcast_to(chunk[None], (n,) + chunk.shape), axes)


def total(chunks):
    return jnp.sum(chunks.astype(F32), 0).astype(BF)


def gather_weight(shard):
    xl, core = lax.axis_index("xl"), lax.axis_index("core")
    other = swap(shard, "xl")
    pair = jnp.where(xl == 0, jnp.stack([shard, other]), jnp.stack([other, shard]))
    far = swap(pair, "core")
    return jnp.where(core == 0, jnp.stack([pair, far], 1), jnp.stack([far, pair], 1)).reshape(D, D)


def reduce_weight_grad(part):
    core = lax.axis_index("core")
    quarters = part.reshape(2, 2, SHARD, D)
    send = lax.dynamic_index_in_dim(quarters, 1 - core, 1, False)
    keep = lax.dynamic_index_in_dim(quarters, core, 1, False)
    halves = (keep.astype(F32) + swap(send, "core").astype(F32)).astype(BF)
    mine = total(exchange(halves.reshape(8, SUB, D), ("xl",) + NEAR))
    tiles = mine.reshape(SUB, 9, 128).transpose(1, 0, 2).reshape(SUB * 9, 128)
    tiles = jnp.pad(tiles, ((0, 768 - SUB * 9), (0, 0))).reshape(32, 24, 128)
    done = total(exchange(tiles, FAR))
    done = spread(done, FAR, 32).reshape(768, 128)[:704]
    done = spread(done, NEAR, 4)[:, : SUB * 9]
    return done.reshape(4, 9, SUB, 128).transpose(0, 2, 1, 3).reshape(SHARD, D).astype(F32)


def with_ids(block, ids):
    row = jnp.pad(ids.astype(BF)[None, :], ((0, 15), (0, D - ROWS)))
    return jnp.concatenate([block, row], 0)


def split_ids(payload):
    return payload[:ROWS], payload[ROWS, :ROWS]


def normalize(rows):
    radius = jnp.sqrt(jnp.sum(rows * rows, -1, keepdims=True) + 1e-06)
    return rows / radius, radius


def on_device(feats, proj_weight, text_embed, row_ids, logit_scale, logit_bias):
    scale = logit_scale[0]
    bias = logit_bias[0]
    payloads = [with_ids(feats, row_ids)]
    payloads.append(shift(payloads[0], -1))
    text_unit = normalize(text_embed.astype(F32))[0].astype(BF)
    text_payload = shift(with_ids(text_unit, row_ids), 1)
    weight = gather_weight(proj_weight)
    payloads.append(shift(payloads[1], -1))
    payloads.append(shift(payloads[2], -1))
    texts = [split_ids(with_ids(text_unit, row_ids)), split_ids(text_payload)]

    def pair(image_unit, ids, text, text_ids):
        logits = (
            scale
            * lax.dot_general(image_unit, text, (((1,), (1,)), ((), ())), preferred_element_type=F32)
            + bias
        )
        sign = jnp.where(ids[:, None] == text_ids[None, :], 1.0, -1.0).astype(F32)
        return (-sign * jax.nn.sigmoid(-sign * logits)).astype(BF)

    text_grad = jnp.zeros((ROWS, D), F32)
    part = jnp.zeros((D, D), F32)
    for offset in range(4):
        columns, ids = split_ids(payloads[offset])
        raw = jnp.dot(columns, weight, preferred_element_type=F32)
        unit, radius = normalize(raw)
        image_unit = unit.astype(BF)
        near = pair(image_unit, ids, *texts[0])
        text_grad = text_grad + scale * lax.dot_general(
            near, image_unit, (((0,), (0,)), ((), ())), preferred_element_type=F32
        )
        if offset < 3:
            back = pair(image_unit, ids, *texts[1])
            image_grad = scale * jnp.dot(back, texts[1][0], preferred_element_type=F32)
            if offset == 0:
                image_grad = image_grad + scale * jnp.dot(near, texts[0][0], preferred_element_type=F32)
            inner = jnp.sum(image_grad * unit, -1, keepdims=True)
            raw_grad = ((image_grad - unit * inner) / radius).astype(BF)
            part = part + lax.dot_general(
                columns, raw_grad, (((0,), (0,)), ((), ())), preferred_element_type=F32
            )
    return (reduce_weight_grad(part.astype(BF)), text_grad)


def solution(mesh):
    fine = Mesh(mesh.devices.reshape((2,) * 9), SPLIT)
    grp = SPLIT[7:]
    return jax.shard_map(
        on_device,
        mesh=fine,
        in_specs=(P(SPLIT, None), P(grp, None), P(SPLIT, None), P(SPLIT), P(), P()),
        out_specs=(P(grp, None), P(SPLIT, None)),
        check_vma=False,
    )
```

```python
import functools

import jax
import jax.numpy as jnp
from jax import lax
from jax.experimental import pallas as pl
from jax.experimental.pallas import tpu as pltpu
from jax.sharding import Mesh, PartitionSpec as P

BF = jnp.bfloat16
F32 = jnp.float32
ROWS = 256
D = 1152
SHARD = D // 4
SUB = SHARD // 4
PACKED = ROWS + 16
SPLIT = ("z2", "z1", "z0", "xh", "y2", "y1", "y0", "xl", "core")
BLK = SPLIT[:7]
NEAR = ("z0", "y0")
FAR = ("z2", "z1", "xh", "y2", "y1")
VMEM = pl.BlockSpec(memory_space=pltpu.VMEM)
SMEM = pl.BlockSpec(memory_space=pltpu.SMEM)


def shift(block, distance):
    n = 128
    return lax.ppermute(block, BLK, [((i - distance) % n, i) for i in range(n)])


def swap(block, axis):
    return lax.ppermute(block, axis, [(0, 1), (1, 0)])


def exchange(chunks, axes):
    return lax.all_to_all(chunks, axes, 0, 0, tiled=True)


def spread(chunk, axes, n):
    return exchange(jnp.broadcast_to(chunk[None], (n,) + chunk.shape), axes)


def total(chunks):
    return jnp.sum(chunks.astype(F32), 0).astype(BF)


def gather_weight(shard, after):
    xl, core = lax.axis_index("xl"), lax.axis_index("core")
    other = swap(shard, "xl")
    pair = jnp.where(xl == 0, jnp.stack([shard, other]), jnp.stack([other, shard]))
    pair = lax.optimization_barrier((pair, after))[0]
    far = swap(pair, "core")
    return jnp.where(core == 0, jnp.stack([pair, far], 1), jnp.stack([far, pair], 1)).reshape(D, D)


def call(kernel, outs, specs, flops, scratch=()):
    def run(*args):
        moved = sum(a.size * a.dtype.itemsize for a in args) + sum(
            o.size * o.dtype.itemsize for o in outs
        )
        return pl.pallas_call(
            kernel,
            out_shape=outs,
            in_specs=specs,
            out_specs=[VMEM] * len(outs),
            scratch_shapes=scratch,
            compiler_params=pltpu.CompilerParams(vmem_limit_bytes=48 * 1024 * 1024),
            cost_estimate=pl.CostEstimate(flops=flops, bytes_accessed=moved, transcendentals=0),
        )(*args)

    return run


def put_ids(ids_ref, out_ref):
    first = lax.broadcasted_iota(jnp.int32, (16, ROWS), 0) == 0
    ids = jnp.broadcast_to(ids_ref[...].astype(F32), (16, ROWS))
    out_ref[ROWS:, :ROWS] = jnp.where(first, ids, 0.0).astype(BF)
    out_ref[ROWS:, ROWS:] = jnp.zeros((16, D - ROWS), BF)


def pack_kernel(feats_ref, ids_ref, out_ref):
    out_ref[:ROWS, :] = feats_ref[...]
    put_ids(ids_ref, out_ref)


def text_kernel(text_ref, ids_ref, out_ref):
    rows = text_ref[...].astype(F32)
    inverse = 1.0 / jnp.sqrt(jnp.sum(rows * rows, -1, keepdims=True) + 1e-06)
    out_ref[:ROWS, :] = (rows * inverse).astype(BF)
    put_ids(ids_ref, out_ref)


def project(image_ref, weight_ref):
    raw = jnp.dot(image_ref[:ROWS, :], weight_ref[...], preferred_element_type=F32)
    inverse = 1.0 / jnp.sqrt(jnp.sum(raw * raw, -1, keepdims=True) + 1e-06)
    unit = raw * inverse
    return unit, unit.astype(BF), inverse


def ids_down(image_ref):
    ones = jnp.ones((16, ROWS), BF)
    return lax.dot_general(
        image_ref[ROWS:, :ROWS], ones, (((0,), (0,)), ((), ())), preferred_element_type=F32
    )


def pair(image_unit, ids, text_ref, scale, bias):
    logits = (
        scale
        * lax.dot_general(
            image_unit, text_ref[:ROWS, :], (((1,), (1,)), ((), ())), preferred_element_type=F32
        )
        + bias
    )
    match = ids == text_ref[ROWS:, :ROWS].astype(F32)[0:1, :]
    weight = 1.0 / (1.0 + jnp.exp(jnp.where(match, logits, -logits)))
    return jnp.where(match, -weight, weight).astype(BF)


def across(left, right):
    return lax.dot_general(left, right, (((0,), (0,)), ((), ())), preferred_element_type=F32)


def back(image_grad, unit, inverse):
    inner = jnp.sum(image_grad * unit, -1, keepdims=True)
    return ((image_grad - unit * inner) * inverse).astype(BF)


def front_kernel(scale_ref, bias_ref, weight_ref, image0_ref, image1_ref, text_ref, text1_ref, part_ref, grad_ref):
    scale, bias = scale_ref[0], bias_ref[0]
    unit, image_unit, inverse = project(image0_ref, weight_ref)
    ids = ids_down(image0_ref)
    near = pair(image_unit, ids, text_ref, scale, bias)
    far = pair(image_unit, ids, text1_ref, scale, bias)
    grad = across(near, image_unit)
    image_grad = scale * (
        jnp.dot(near, text_ref[:ROWS, :], preferred_element_type=F32)
        + jnp.dot(far, text1_ref[:ROWS, :], preferred_element_type=F32)
    )
    part_ref[...] = across(image0_ref[:ROWS, :], back(image_grad, unit, inverse))
    unit, image_unit, inverse = project(image1_ref, weight_ref)
    ids = ids_down(image1_ref)
    near = pair(image_unit, ids, text_ref, scale, bias)
    far = pair(image_unit, ids, text1_ref, scale, bias)
    grad_ref[...] = scale * (grad + across(near, image_unit))
    image_grad = scale * jnp.dot(far, text1_ref[:ROWS, :], preferred_element_type=F32)
    part_ref[...] += across(image1_ref[:ROWS, :], back(image_grad, unit, inverse))


def last_kernel(core_ref, scale_ref, bias_ref, weight_ref, image_ref, text1_ref, part_ref, keep_ref, send_ref, sum_ref, sem):
    scale, bias = scale_ref[0], bias_ref[0]
    load = pltpu.make_async_copy(part_ref, sum_ref, sem)
    load.start()
    unit, image_unit, inverse = project(image_ref, weight_ref)
    far = pair(image_unit, ids_down(image_ref), text1_ref, scale, bias)
    image_grad = scale * jnp.dot(far, text1_ref[:ROWS, :], preferred_element_type=F32)
    raw_grad = back(image_grad, unit, inverse)
    load.wait()
    sum_ref[...] += across(image_ref[:ROWS, :], raw_grad)
    core = core_ref[0]
    for half in range(2):
        for out_ref, quarter in ((keep_ref, core), (send_ref, 1 - core)):
            at = pl.multiple_of((2 * half + quarter) * SHARD, 32)
            out_ref[half * SHARD : (half + 1) * SHARD, :] = sum_ref[pl.ds(at, SHARD), :].astype(BF)


def finish_kernel(scale_ref, bias_ref, weight_ref, image2_ref, image3_ref, text_ref, grad_ref, out_ref):
    scale, bias = scale_ref[0], bias_ref[0]
    grad = None
    for image_ref in (image2_ref, image3_ref):
        _, image_unit, _ = project(image_ref, weight_ref)
        near = pair(image_unit, ids_down(image_ref), text_ref, scale, bias)
        term = across(near, image_unit)
        grad = term if grad is None else grad + term
    out_ref[...] = grad_ref[...] + scale * grad


def shape(rows, columns, dtype):
    return jax.ShapeDtypeStruct((rows, columns), dtype)


def on_device(feats, proj_weight, text_embed, row_ids, logit_scale, logit_bias):
    ids = row_ids.reshape(1, ROWS)
    packed = shape(PACKED, D, BF)
    core = lax.axis_index("core").astype(jnp.int32).reshape(1)
    image0 = call(pack_kernel, [packed], [VMEM] * 2, ROWS)(feats, ids)[0]
    image0, text_embed = lax.optimization_barrier((image0, text_embed))
    image1 = shift(image0, -1)
    text0 = call(text_kernel, [packed], [VMEM] * 2, ROWS)(text_embed, ids)[0]
    proj_weight, text0 = lax.optimization_barrier((proj_weight, text0))
    text1 = shift(text0, 1)
    weight = gather_weight(proj_weight, (image1, text1))
    image2 = shift(image1, -1)
    project_flops = 2 * ROWS * D * D
    part, grad = call(
        front_kernel,
        [shape(D, D, F32), shape(ROWS, D, F32)],
        [SMEM] * 2 + [VMEM] * 5,
        4 * project_flops,
    )(logit_scale, logit_bias, weight, image0, image1, text0, text1)
    keep, send = call(
        last_kernel,
        [shape(2 * SHARD, D, BF)] * 2,
        [SMEM] * 3 + [VMEM] * 3 + [pl.BlockSpec(memory_space=pl.ANY)],
        2 * project_flops,
        [pltpu.VMEM((D, D), F32), pltpu.SemaphoreType.DMA],
    )(core, logit_scale, logit_bias, weight, image2, text1, part)
    halves = (keep.astype(F32) + swap(send, "core").astype(F32)).astype(BF)
    mine = total(exchange(halves.reshape(8, SUB, D), ("xl",) + NEAR))
    mine, image2 = lax.optimization_barrier((mine, image2))
    tiles = mine.reshape(SUB, 9, 128).transpose(1, 0, 2).reshape(SUB * 9, 128)
    tiles = jnp.pad(tiles, ((0, 768 - SUB * 9), (0, 0))).reshape(32, 24, 128)
    done = total(exchange(tiles, FAR))
    image3 = shift(image2, -1)
    done = spread(done, FAR, 32).reshape(768, 128)[:704]
    done, image3 = lax.optimization_barrier((done, image3))
    done = spread(done, NEAR, 4)[:, : SUB * 9]
    weight_grad = done.reshape(4, 9, SUB, 128).transpose(0, 2, 1, 3).reshape(SHARD, D).astype(F32)
    text_grad = call(
        finish_kernel, [shape(ROWS, D, F32)], [SMEM] * 2 + [VMEM] * 5, 2 * project_flops
    )(logit_scale, logit_bias, weight, image2, image3, text0, grad)[0]
    return (weight_grad, text_grad)


def solution(mesh):
    fine = Mesh(mesh.devices.reshape((2,) * 9), SPLIT)
    grp = SPLIT[7:]
    return jax.shard_map(
        on_device,
        mesh=fine,
        in_specs=(P(SPLIT, None), P(grp, None), P(SPLIT, None), P(SPLIT), P(), P()),
        out_specs=(P(grp, None), P(SPLIT, None)),
        check_vma=False,
    )
```

```python
import jax
import jax.numpy as jnp
from jax import lax
from jax.experimental import pallas as pl
from jax.experimental.pallas import tpu as pltpu
from jax.sharding import PartitionSpec as P

BF = jnp.bfloat16
F32 = jnp.float32
ROWS = 256
D = 1152
SHARD = D // 4
SUB = SHARD // 4
PACKED = ROWS + 16
N = 512
AXIS = ("blk", "grp")
VMEM = pl.BlockSpec(memory_space=pltpu.VMEM)
SMEM = pl.BlockSpec(memory_space=pltpu.SMEM)


def coordinates(device):
    blk, grp = divmod(device, 4)
    return blk // 16, (blk // 8) % 2 * 2 + grp // 2, blk % 8, grp % 2


def device_at(z, x, y, core):
    return ((z % 8 * 2 + x % 4 // 2) * 8 + y % 8) * 4 + x % 2 * 2 + core


def swap_x(flips):
    moves = []
    for device in range(N):
        z, x, y, core = coordinates(device)
        moves.append((device_at(z, x ^ flips[core], y, core), device))
    return moves


def grouped(same, place):
    groups = {}
    for device in range(N):
        z, x, y, core = coordinates(device)
        key = (z + core) % 8, (x + core) % 4, (y + core) % 8, x % 2, core
        groups.setdefault(same(*key), []).append((place(*key), device))
    return [[device for _, device in sorted(group)] for group in groups.values()]


FIRST = grouped(lambda z, x, y, xl, core: (z // 2, x // 2, y // 2, core), lambda z, x, y, xl, core: (xl, z % 2, y % 2))
NEAR = grouped(lambda z, x, y, xl, core: (z // 2, x, y // 2, core), lambda z, x, y, xl, core: (z % 2, y % 2))
FAR = grouped(lambda z, x, y, xl, core: (z % 2, x, y % 2, core), lambda z, x, y, xl, core: (z // 2, y // 2))
CORES = [(i ^ 1, i) for i in range(N)]


def shift(block, distance):
    return lax.ppermute(block, AXIS, [((i - 4 * distance) % N, i) for i in range(N)])


def move(block, moves):
    return lax.ppermute(block, AXIS, moves)


def exchange(chunks, groups):
    return lax.all_to_all(chunks, AXIS, 0, 0, axis_index_groups=groups, tiled=True)


def spread(chunk, groups):
    return exchange(jnp.broadcast_to(chunk[None], (len(groups[0]),) + chunk.shape), groups)


def total(chunks):
    return jnp.sum(chunks.astype(F32), 0).astype(BF)


def call(kernel, outs, specs, flops, scratch=()):
    def run(*args):
        moved = sum(a.size * a.dtype.itemsize for a in args) + sum(
            o.size * o.dtype.itemsize for o in outs
        )
        return pl.pallas_call(
            kernel,
            out_shape=outs,
            in_specs=specs,
            out_specs=[VMEM] * len(outs),
            scratch_shapes=scratch,
            compiler_params=pltpu.CompilerParams(vmem_limit_bytes=48 * 1024 * 1024),
            cost_estimate=pl.CostEstimate(flops=flops, bytes_accessed=moved, transcendentals=0),
        )(*args)

    return run


def put_ids(ids_ref, out_ref):
    first = lax.broadcasted_iota(jnp.int32, (16, ROWS), 0) == 0
    ids = jnp.broadcast_to(ids_ref[...].astype(F32), (16, ROWS))
    out_ref[ROWS:, :ROWS] = jnp.where(first, ids, 0.0).astype(BF)
    out_ref[ROWS:, ROWS:] = jnp.zeros((16, D - ROWS), BF)


def prepare_kernel(feats_ref, text_ref, ids_ref, image_ref, out_ref):
    image_ref[:ROWS, :] = feats_ref[...]
    put_ids(ids_ref, image_ref)
    rows = text_ref[...].astype(F32)
    inverse = 1.0 / jnp.sqrt(jnp.sum(rows * rows, -1, keepdims=True) + 1e-06)
    out_ref[:ROWS, :] = (rows * inverse).astype(BF)
    put_ids(ids_ref, out_ref)


def project(image_ref, weight_ref):
    raw = jnp.dot(image_ref[:ROWS, :], weight_ref[...], preferred_element_type=F32)
    inverse = 1.0 / jnp.sqrt(jnp.sum(raw * raw, -1, keepdims=True) + 1e-06)
    unit = raw * inverse
    return unit, unit.astype(BF), inverse


def ids_down(image_ref):
    ones = jnp.ones((16, ROWS), BF)
    return lax.dot_general(
        image_ref[ROWS:, :ROWS], ones, (((0,), (0,)), ((), ())), preferred_element_type=F32
    )


def pair(image_unit, ids, text_ref, scale, bias):
    logits = (
        scale
        * lax.dot_general(
            image_unit, text_ref[:ROWS, :], (((1,), (1,)), ((), ())), preferred_element_type=F32
        )
        + bias
    )
    match = ids == text_ref[ROWS:, :ROWS].astype(F32)[0:1, :]
    weight = 1.0 / (1.0 + jnp.exp(jnp.where(match, logits, -logits)))
    return jnp.where(match, -weight, weight).astype(BF)


def across(left, right):
    return lax.dot_general(left, right, (((0,), (0,)), ((), ())), preferred_element_type=F32)


def back(image_grad, unit, inverse):
    inner = jnp.sum(image_grad * unit, -1, keepdims=True)
    return ((image_grad - unit * inner) * inverse).astype(BF)


def own_kernel(
    grp_ref, scale_ref, bias_ref, shard0_ref, shard1_ref, shard2_ref, shard3_ref, image_ref, text_ref, weight_ref, raw_grad_ref, grad_ref
):
    grp = grp_ref[0]
    for flip, shard_ref in enumerate((shard0_ref, shard1_ref, shard2_ref, shard3_ref)):
        weight_ref[pl.ds(pl.multiple_of((grp ^ flip) * SHARD, 32), SHARD), :] = shard_ref[...]
    scale, bias = scale_ref[0], bias_ref[0]
    unit, image_unit, inverse = project(image_ref, weight_ref)
    near = pair(image_unit, ids_down(image_ref), text_ref, scale, bias)
    grad_ref[...] = across(near, image_unit)
    image_grad = scale * jnp.dot(near, text_ref[:ROWS, :], preferred_element_type=F32)
    raw_grad_ref[...] = back(image_grad, unit, inverse)


def next_kernel(
    scale_ref, bias_ref, weight_ref, image0_ref, raw_grad0_ref, image1_ref, text_ref, text1_ref, grad0_ref, part_ref, grad_ref
):
    scale, bias = scale_ref[0], bias_ref[0]
    unit, image_unit, inverse = project(image1_ref, weight_ref)
    ids = ids_down(image1_ref)
    near = pair(image_unit, ids, text_ref, scale, bias)
    far = pair(image_unit, ids, text1_ref, scale, bias)
    grad_ref[...] = grad0_ref[...] + across(near, image_unit)
    image_grad = scale * (
        jnp.dot(near, text_ref[:ROWS, :], preferred_element_type=F32)
        + jnp.dot(far, text1_ref[:ROWS, :], preferred_element_type=F32)
    )
    raw_grad = back(image_grad, unit, inverse)
    part_ref[...] = across(image0_ref[:ROWS, :], raw_grad0_ref[...])
    part_ref[...] += across(image1_ref[:ROWS, :], raw_grad)


def load_quarters(core, part_ref, rows_ref, sems):
    loads = []
    for half in range(2):
        at = pl.multiple_of((2 * half + core) * SHARD, 32)
        loads.append(
            pltpu.make_async_copy(
                part_ref.at[pl.ds(at, SHARD), :],
                rows_ref.at[pl.ds(half * SHARD, SHARD), :],
                sems.at[half],
            )
        )
    for load in loads:
        load.start()
    return loads


def add_quarters(core, turned_ref, raw_grad, rows_ref, loads, out_ref):
    for half in range(2):
        at = pl.multiple_of((2 * half + core) * SHARD, 32)
        rows = pl.ds(half * SHARD, SHARD)
        term = jnp.dot(turned_ref[pl.ds(at, SHARD), :], raw_grad, preferred_element_type=F32)
        loads[half].wait()
        out_ref[rows, :] = (rows_ref[rows, :] + term).astype(BF)


def last_kernel(
    grp_ref, scale_ref, bias_ref, weight_ref, image_ref, text1_ref, part_ref, send_ref, turned_ref, raw_grad_ref, rows_ref, sems
):
    core = 1 - grp_ref[0] % 2
    loads = load_quarters(core, part_ref, rows_ref, sems)
    scale, bias = scale_ref[0], bias_ref[0]
    turned_ref[...] = image_ref[:ROWS, :].astype(F32).T.astype(BF)
    unit, image_unit, inverse = project(image_ref, weight_ref)
    far = pair(image_unit, ids_down(image_ref), text1_ref, scale, bias)
    image_grad = scale * jnp.dot(far, text1_ref[:ROWS, :], preferred_element_type=F32)
    raw_grad = back(image_grad, unit, inverse)
    raw_grad_ref[...] = raw_grad
    add_quarters(core, turned_ref, raw_grad, rows_ref, loads, send_ref)


def keep_kernel(grp_ref, turned_ref, raw_grad_ref, part_ref, keep_ref, rows_ref, sems):
    core = grp_ref[0] % 2
    loads = load_quarters(core, part_ref, rows_ref, sems)
    add_quarters(core, turned_ref, raw_grad_ref[...], rows_ref, loads, keep_ref)


def finish_kernel(scale_ref, bias_ref, weight_ref, image2_ref, image3_ref, text_ref, grad_ref, out_ref):
    scale, bias = scale_ref[0], bias_ref[0]
    grad = None
    for image_ref in (image2_ref, image3_ref):
        _, image_unit, _ = project(image_ref, weight_ref)
        near = pair(image_unit, ids_down(image_ref), text_ref, scale, bias)
        term = across(near, image_unit)
        grad = term if grad is None else grad + term
    out_ref[...] = scale * (grad_ref[...] + grad)


def shape(rows, columns, dtype):
    return jax.ShapeDtypeStruct((rows, columns), dtype)


def on_device(feats, proj_weight, text_embed, row_ids, logit_scale, logit_bias):
    packed = shape(PACKED, D, BF)
    grp = lax.axis_index("grp").astype(jnp.int32).reshape(1)
    numbers = (logit_scale, logit_bias)
    flops = 2 * ROWS * D * D
    anywhere = pl.BlockSpec(memory_space=pl.ANY)
    scratch = [pltpu.VMEM((2 * SHARD, D), F32), pltpu.SemaphoreType.DMA((2,))]
    image0, text0 = call(prepare_kernel, [packed] * 2, [VMEM] * 3, ROWS)(
        feats, text_embed, row_ids.reshape(1, ROWS)
    )
    shard1 = move(proj_weight, CORES)
    shard2 = move(proj_weight, swap_x((1, 3)))
    image1 = shift(image0, -1)
    text1 = shift(text0, 1)
    image2 = shift(image1, -1)
    shard2, text1 = lax.optimization_barrier((shard2, text1))
    shard3 = move(shard2, CORES)
    weight, raw_grad0, grad = call(
        own_kernel, [shape(D, D, BF), shape(ROWS, D, BF), shape(ROWS, D, F32)], [SMEM] * 3 + [VMEM] * 6, flops
    )(grp, *numbers, proj_weight, shard1, shard2, shard3, image0, text0)
    part, grad = call(
        next_kernel, [shape(D, D, F32), shape(ROWS, D, F32)], [SMEM] * 2 + [VMEM] * 7, 4 * flops
    )(*numbers, weight, image0, raw_grad0, image1, text0, text1, grad)
    send, turned, raw_grad2 = call(
        last_kernel,
        [shape(2 * SHARD, D, BF), shape(D, ROWS, BF), shape(ROWS, D, BF)],
        [SMEM] * 3 + [VMEM] * 3 + [anywhere],
        2 * flops,
        scratch,
    )(grp, *numbers, weight, image2, text1, part)
    keep = call(
        keep_kernel, [shape(2 * SHARD, D, BF)], [SMEM] + [VMEM] * 2 + [anywhere], flops, scratch
    )(grp, turned, raw_grad2, part)[0]
    halves = (keep.astype(F32) + move(send, CORES).astype(F32)).astype(BF)
    mine = total(exchange(halves.reshape(8, SUB, D), FIRST))
    mine, image2 = lax.optimization_barrier((mine, image2))
    tiles = mine.reshape(SUB, 9, 128).transpose(1, 0, 2).reshape(SUB * 9, 128)
    tiles = jnp.pad(tiles, ((0, 768 - SUB * 9), (0, 0))).reshape(16, 48, 128)
    done = total(exchange(tiles, FAR))
    image3 = shift(image2, -1)
    done = (done.astype(F32) + move(done, swap_x((2, 2))).astype(F32)).astype(BF)
    done = spread(done, FAR).reshape(768, 128)[:704]
    done, image3 = lax.optimization_barrier((done, image3))
    done = spread(done, NEAR)[:, : SUB * 9]
    weight_grad = done.reshape(4, 9, SUB, 128).transpose(0, 2, 1, 3).reshape(SHARD, D).astype(F32)
    text_grad = call(finish_kernel, [shape(ROWS, D, F32)], [SMEM] * 2 + [VMEM] * 5, 2 * flops)(
        *numbers, weight, image2, image3, text0, grad
    )[0]
    return (weight_grad, text_grad)


def solution(mesh):
    return jax.shard_map(
        on_device,
        mesh=mesh,
        in_specs=(P(AXIS, None), P("grp", None), P(AXIS, None), P(AXIS), P(), P()),
        out_specs=(P("grp", None), P(AXIS, None)),
        check_vma=False,
    )
```

```python
import jax
import jax.numpy as jnp
from jax import lax
from jax.experimental import pallas as pl
from jax.experimental.pallas import tpu as pltpu
from jax.sharding import PartitionSpec as P

BF = jnp.bfloat16
F32 = jnp.float32
ROWS = 256
D = 1152
SHARD = D // 4
SUB = SHARD // 4
PACKED = ROWS + 16
N = 512
AXIS = ("blk", "grp")
VMEM = pl.BlockSpec(memory_space=pltpu.VMEM)
SMEM = pl.BlockSpec(memory_space=pltpu.SMEM)


def coordinates(device):
    blk, grp = divmod(device, 4)
    return blk // 16, (blk // 8) % 2 * 2 + grp // 2, blk % 8, grp % 2


def device_at(z, x, y, core):
    return ((z % 8 * 2 + x % 4 // 2) * 8 + y % 8) * 4 + x % 2 * 2 + core


def swap_x(flips):
    moves = []
    for device in range(N):
        z, x, y, core = coordinates(device)
        moves.append((device_at(z, x ^ flips[core], y, core), device))
    return moves


def grouped(same, place):
    groups = {}
    for device in range(N):
        z, x, y, core = coordinates(device)
        key = (z + core) % 8, (x + core) % 4, (y + core) % 8, x % 2, core
        groups.setdefault(same(*key), []).append((place(*key), device))
    return [[device for _, device in sorted(group)] for group in groups.values()]


FIRST = grouped(lambda z, x, y, xl, core: (z // 2, x // 2, y // 2, core), lambda z, x, y, xl, core: (xl, z % 2, y % 2))
NEAR = grouped(lambda z, x, y, xl, core: (z // 2, x, y // 2, core), lambda z, x, y, xl, core: (z % 2, y % 2))
FAR = grouped(lambda z, x, y, xl, core: (z % 2, x, y % 2, core), lambda z, x, y, xl, core: (z // 2, y // 2))
CORES = [(i ^ 1, i) for i in range(N)]


def shift(block, distance):
    return lax.ppermute(block, AXIS, [((i - 4 * distance) % N, i) for i in range(N)])


def move(block, moves):
    return lax.ppermute(block, AXIS, moves)


def exchange(chunks, groups):
    return lax.all_to_all(chunks, AXIS, 0, 0, axis_index_groups=groups, tiled=True)


def spread(chunk, groups):
    return exchange(jnp.broadcast_to(chunk[None], (len(groups[0]),) + chunk.shape), groups)


def total(chunks):
    return jnp.sum(chunks.astype(F32), 0).astype(BF)


def call(kernel, outs, specs, flops, scratch=()):
    def run(*args):
        moved = sum(a.size * a.dtype.itemsize for a in args) + sum(
            o.size * o.dtype.itemsize for o in outs
        )
        return pl.pallas_call(
            kernel,
            out_shape=outs,
            in_specs=specs,
            out_specs=[VMEM] * len(outs),
            scratch_shapes=scratch,
            compiler_params=pltpu.CompilerParams(vmem_limit_bytes=20 * 1024 * 1024),
            cost_estimate=pl.CostEstimate(flops=flops, bytes_accessed=moved, transcendentals=0),
        )(*args)

    return run


def top_row(ids_ref):
    first = lax.broadcasted_iota(jnp.int32, (16, ROWS), 0) == 0
    ids = jnp.broadcast_to(ids_ref[...].astype(F32), (16, ROWS))
    return jnp.where(first, ids, 0.0).astype(BF)


def prepare_kernel(text_ref, ids_ref, out_ref):
    rows = text_ref[...].astype(F32)
    inverse = 1.0 / jnp.sqrt(jnp.sum(rows * rows, -1, keepdims=True) + 1e-06)
    out_ref[:ROWS, :] = (rows * inverse).astype(BF)
    out_ref[ROWS:, :ROWS] = top_row(ids_ref)
    out_ref[ROWS:, ROWS:] = jnp.zeros((16, D - ROWS), BF)


def project(image_ref, weight_ref):
    raw = jnp.dot(image_ref[...], weight_ref[...], preferred_element_type=F32)
    inverse = 1.0 / jnp.sqrt(jnp.sum(raw * raw, -1, keepdims=True) + 1e-06)
    unit = raw * inverse
    return unit, unit.astype(BF), inverse


def ids_down(ids_ref):
    return across(top_row(ids_ref), jnp.ones((16, ROWS), BF))


def turn(image_ref):
    return image_ref[...].astype(F32).T.astype(BF)


def pair(image_unit, ids, text_ref, scale, bias):
    logits = (
        scale
        * lax.dot_general(
            image_unit, text_ref[:ROWS, :], (((1,), (1,)), ((), ())), preferred_element_type=F32
        )
        + bias
    )
    match = ids == text_ref[ROWS:, :ROWS].astype(F32)[0:1, :]
    weight = 1.0 / (1.0 + jnp.exp(jnp.where(match, logits, -logits)))
    return jnp.where(match, -weight, weight).astype(BF)


def across(left, right):
    return lax.dot_general(left, right, (((0,), (0,)), ((), ())), preferred_element_type=F32)


def back(image_grad, unit, inverse):
    inner = jnp.sum(image_grad * unit, -1, keepdims=True)
    return ((image_grad - unit * inner) * inverse).astype(BF)


def own_kernel(
    grp_ref, scale_ref, bias_ref, shard0_ref, shard1_ref, shard2_ref, shard3_ref, image_ref, ids_ref, text_ref, weight_ref, raw_grad_ref, grad_ref, sems
):
    grp = grp_ref[0]
    loads = []
    for flip, shard_ref in enumerate((shard0_ref, shard1_ref, shard2_ref, shard3_ref)):
        rows = pl.ds(pl.multiple_of((grp ^ flip) * SHARD, 32), SHARD)
        loads.append(pltpu.make_async_copy(shard_ref, weight_ref.at[rows, :], sems.at[flip]))
        loads[-1].start()
    for load in loads:
        load.wait()
    scale, bias = scale_ref[0], bias_ref[0]
    unit, image_unit, inverse = project(image_ref, weight_ref)
    near = pair(image_unit, ids_down(ids_ref), text_ref, scale, bias)
    grad_ref[...] = across(near, image_unit)
    image_grad = scale * jnp.dot(near, text_ref[:ROWS, :], preferred_element_type=F32)
    raw_grad_ref[...] = back(image_grad, unit, inverse)


def next_kernel(
    scale_ref, bias_ref, weight_ref, image0_ref, raw_grad0_ref, image1_ref, ids_ref, text_ref, text1_ref, grad0_ref, part_ref, grad_ref,
    turned_ref, raw_grads_ref
):
    turned_ref[:, :ROWS] = turn(image0_ref)
    turned_ref[:, ROWS:] = turn(image1_ref)
    raw_grads_ref[:ROWS, :] = raw_grad0_ref[...]
    scale, bias = scale_ref[0], bias_ref[0]
    unit, image_unit, inverse = project(image1_ref, weight_ref)
    ids = ids_down(ids_ref)
    near = pair(image_unit, ids, text_ref, scale, bias)
    far = pair(image_unit, ids, text1_ref, scale, bias)
    grad_ref[...] = grad0_ref[...] + across(near, image_unit)
    image_grad = scale * (
        jnp.dot(near, text_ref[:ROWS, :], preferred_element_type=F32)
        + jnp.dot(far, text1_ref[:ROWS, :], preferred_element_type=F32)
    )
    raw_grads_ref[ROWS:, :] = back(image_grad, unit, inverse)
    part_ref[...] = jnp.dot(turned_ref[...], raw_grads_ref[...], preferred_element_type=F32)


def load_quarters(core, part_ref, rows_ref, sems):
    loads = []
    for half in range(2):
        at = pl.multiple_of((2 * half + core) * SHARD, 32)
        loads.append(
            pltpu.make_async_copy(
                part_ref.at[pl.ds(at, SHARD), :],
                rows_ref.at[pl.ds(half * SHARD, SHARD), :],
                sems.at[half],
            )
        )
    for load in loads:
        load.start()
    return loads


def add_quarters(core, turned_ref, raw_grad, rows_ref, loads, out_ref):
    for half in range(2):
        at = pl.multiple_of((2 * half + core) * SHARD, 32)
        rows = pl.ds(half * SHARD, SHARD)
        term = jnp.dot(turned_ref[pl.ds(at, SHARD), :], raw_grad, preferred_element_type=F32)
        loads[half].wait()
        out_ref[rows, :] = (rows_ref[rows, :] + term).astype(BF)


def last_kernel(
    grp_ref, scale_ref, bias_ref, weight_ref, image_ref, ids_ref, text1_ref, part_ref,
    send_ref, turned_ref, raw_grad_ref, image_unit_ref, far_ref, rows_ref, sems
):
    core = 1 - grp_ref[0] % 2
    loads = load_quarters(core, part_ref, rows_ref, sems)
    scale, bias = scale_ref[0], bias_ref[0]
    turned_ref[...] = turn(image_ref)
    unit, image_unit, inverse = project(image_ref, weight_ref)
    image_unit_ref[...] = image_unit
    far = pair(image_unit, ids_down(ids_ref), text1_ref, scale, bias)
    far_ref[...] = far
    image_grad = scale * jnp.dot(far, text1_ref[:ROWS, :], preferred_element_type=F32)
    raw_grad = back(image_grad, unit, inverse)
    raw_grad_ref[...] = raw_grad
    add_quarters(core, turned_ref, raw_grad, rows_ref, loads, send_ref)


def keep_kernel(grp_ref, turned_ref, raw_grad_ref, image_unit_ref, far_ref, part_ref, keep_ref, back_ref, rows_ref, sems):
    core = grp_ref[0] % 2
    loads = load_quarters(core, part_ref, rows_ref, sems)
    add_quarters(core, turned_ref, raw_grad_ref[...], rows_ref, loads, keep_ref)
    back_ref[...] = across(far_ref[...], image_unit_ref[...]).astype(BF)


def finish_kernel(scale_ref, bias_ref, image_unit2_ref, ids2_ref, text_ref, grad_ref, back_ref, out_ref):
    image_unit2 = image_unit2_ref[...]
    near2 = pair(image_unit2, ids_down(ids2_ref), text_ref, scale_ref[0], bias_ref[0])
    out_ref[...] = scale_ref[0] * (grad_ref[...] + across(near2, image_unit2) + back_ref[...].astype(F32))


def shape(rows, columns, dtype):
    return jax.ShapeDtypeStruct((rows, columns), dtype)


def on_device(feats, proj_weight, text_embed, row_ids, logit_scale, logit_bias):
    packed = shape(PACKED, D, BF)
    grp = lax.axis_index("grp").astype(jnp.int32).reshape(1)
    numbers = (logit_scale, logit_bias)
    flops = 2 * ROWS * D * D
    anywhere = pl.BlockSpec(memory_space=pl.ANY)
    scratch = [pltpu.VMEM((2 * SHARD, D), F32), pltpu.SemaphoreType.DMA((2,))]
    ids = [row_ids.reshape(1, ROWS)]
    text0 = call(prepare_kernel, [packed], [VMEM] * 2, ROWS)(text_embed, ids[0])[0]
    shard1 = move(proj_weight, CORES)
    shard2 = move(proj_weight, swap_x((1, 3)))
    image1 = shift(feats, -1)
    text1 = shift(text0, 1)
    image2 = shift(image1, -1)
    late_ids = lax.optimization_barrier((row_ids, shard2))[0]
    ids += [shift(late_ids, -distance).reshape(1, ROWS) for distance in (1, 2)]
    shard2, text1 = lax.optimization_barrier((shard2, text1))
    shard3 = move(shard2, CORES)
    weight, raw_grad0, grad = call(
        own_kernel, [shape(D, D, BF), shape(ROWS, D, BF), shape(ROWS, D, F32)], [SMEM] * 3 + [anywhere] * 4 + [VMEM] * 3, flops,
        [pltpu.SemaphoreType.DMA((4,))],
    )(grp, *numbers, proj_weight, shard1, shard2, shard3, feats, ids[0], text0)
    part, grad = call(
        next_kernel,
        [shape(D, D, F32), shape(ROWS, D, F32)],
        [SMEM] * 2 + [VMEM] * 8,
        4 * flops,
        [pltpu.VMEM((D, 2 * ROWS), BF), pltpu.VMEM((2 * ROWS, D), BF)],
    )(*numbers, weight, feats, raw_grad0, image1, ids[1], text0, text1, grad)
    send, turned, raw_grad2, image_unit2, far = call(
        last_kernel,
        [shape(2 * SHARD, D, BF), shape(D, ROWS, BF), shape(ROWS, D, BF), shape(ROWS, D, BF), shape(ROWS, ROWS, BF)],
        [SMEM] * 3 + [VMEM] * 4 + [anywhere],
        2 * flops,
        scratch,
    )(grp, *numbers, weight, image2, ids[2], text1, part)
    keep, term = call(
        keep_kernel,
        [shape(2 * SHARD, D, BF), shape(ROWS, D, BF)],
        [SMEM] + [VMEM] * 4 + [anywhere],
        flops,
        scratch,
    )(grp, turned, raw_grad2, image_unit2, far, part)
    term = shift(term, -1)
    halves = (keep.astype(F32) + move(send, CORES).astype(F32)).astype(BF)
    mine = total(exchange(halves.reshape(8, SUB, D), FIRST))
    mine, term = lax.optimization_barrier((mine, term))
    tiles = mine.reshape(SUB, 9, 128).transpose(1, 0, 2).reshape(SUB * 9, 128)
    tiles = jnp.pad(tiles, ((0, 768 - SUB * 9), (0, 0))).reshape(16, 48, 128)
    done = total(exchange(tiles, FAR))
    done = (done.astype(F32) + move(done, swap_x((2, 2))).astype(F32)).astype(BF)
    done = spread(done, FAR).reshape(768, 128)[:704]
    done = spread(done, NEAR)[:, : SUB * 9]
    weight_grad = done.reshape(4, 9, SUB, 128).transpose(0, 2, 1, 3).reshape(SHARD, D).astype(F32)
    text_grad = call(finish_kernel, [shape(ROWS, D, F32)], [SMEM] * 2 + [VMEM] * 5, flops)(
        *numbers, image_unit2, ids[2], text0, grad, term
    )[0]
    return (weight_grad, text_grad)


def solution(mesh):
    return jax.shard_map(
        on_device,
        mesh=mesh,
        in_specs=(P(AXIS, None), P("grp", None), P(AXIS, None), P(AXIS), P(), P()),
        out_specs=(P("grp", None), P(AXIS, None)),
        check_vma=False,
    )
```

```python
import jax
import jax.numpy as jnp
from jax import lax
from jax.experimental import pallas as pl
from jax.experimental.pallas import tpu as pltpu
from jax.sharding import PartitionSpec as P

BF = jnp.bfloat16
F32 = jnp.float32
ROWS = 256
D = 1152
SHARD = D // 4
SUB = SHARD // 4
PACKED = ROWS + 16
N = 512
AXIS = ("blk", "grp")
VMEM = pl.BlockSpec(memory_space=pltpu.VMEM)
SMEM = pl.BlockSpec(memory_space=pltpu.SMEM)


def coordinates(device):
    blk, grp = divmod(device, 4)
    return blk // 16, (blk // 8) % 2 * 2 + grp // 2, blk % 8, grp % 2


def device_at(z, x, y, core):
    return ((z % 8 * 2 + x % 4 // 2) * 8 + y % 8) * 4 + x % 2 * 2 + core


def swap_x(flips):
    moves = []
    for device in range(N):
        z, x, y, core = coordinates(device)
        moves.append((device_at(z, x ^ flips[core], y, core), device))
    return moves


def grouped(same, place):
    groups = {}
    for device in range(N):
        z, x, y, core = coordinates(device)
        key = (z + core) % 8, (x + core) % 4, (y + core) % 8, x % 2, core
        groups.setdefault(same(*key), []).append((place(*key), device))
    return [[device for _, device in sorted(group)] for group in groups.values()]


FIRST = grouped(lambda z, x, y, xl, core: (z // 2, x // 2, y // 2, core), lambda z, x, y, xl, core: (xl, z % 2, y % 2))
NEAR = grouped(lambda z, x, y, xl, core: (z // 2, x, y // 2, core), lambda z, x, y, xl, core: (z % 2, y % 2))
FAR = grouped(lambda z, x, y, xl, core: (z % 2, x, y % 2, core), lambda z, x, y, xl, core: (z // 2, y // 2))
EVEN, ODD = (
    [[blk * 4 + grp, (blk + 1) * 4 % N + grp] for blk in range(first, 128, 2) for grp in range(4)] for first in range(2)
)
CORES = [(i ^ 1, i) for i in range(N)]


def shift(block, distance):
    return lax.ppermute(block, AXIS, [((i - 4 * distance) % N, i) for i in range(N)])


def move(block, moves):
    return lax.ppermute(block, AXIS, moves)


def exchange(chunks, groups):
    return lax.all_to_all(chunks, AXIS, 0, 0, axis_index_groups=groups, tiled=True)


def spread(chunk, groups):
    return exchange(jnp.broadcast_to(chunk[None], (len(groups[0]),) + chunk.shape), groups)


def total(chunks):
    return jnp.sum(chunks.astype(F32), 0).astype(BF)


def call(kernel, outs, specs, flops, scratch=()):
    def run(*args):
        moved = sum(a.size * a.dtype.itemsize for a in args) + sum(
            o.size * o.dtype.itemsize for o in outs
        )
        return pl.pallas_call(
            kernel,
            out_shape=outs,
            in_specs=specs,
            out_specs=[VMEM] * len(outs),
            scratch_shapes=scratch,
            compiler_params=pltpu.CompilerParams(vmem_limit_bytes=20 * 1024 * 1024),
            cost_estimate=pl.CostEstimate(flops=flops, bytes_accessed=moved, transcendentals=0),
        )(*args)

    return run


def top_row(ids_ref):
    first = lax.broadcasted_iota(jnp.int32, (16, ROWS), 0) == 0
    ids = jnp.broadcast_to(ids_ref[...].astype(F32), (16, ROWS))
    return jnp.where(first, ids, 0.0).astype(BF)


def put_ids(ids_ref, out_ref):
    out_ref[ROWS:, :ROWS] = top_row(ids_ref)
    out_ref[ROWS:, ROWS:] = jnp.zeros((16, D - ROWS), BF)


def pack_kernel(feats_ref, ids_ref, out_ref):
    out_ref[:ROWS, :] = feats_ref[...]
    put_ids(ids_ref, out_ref)


def text_kernel(text_ref, ids_ref, out_ref):
    rows = text_ref[...].astype(F32)
    inverse = 1.0 / jnp.sqrt(jnp.sum(rows * rows, -1, keepdims=True) + 1e-06)
    out_ref[:ROWS, :] = (rows * inverse).astype(BF)
    put_ids(ids_ref, out_ref)


def project(image_ref, weight_ref):
    raw = jnp.dot(image_ref[:ROWS, :], weight_ref[...], preferred_element_type=F32)
    inverse = 1.0 / jnp.sqrt(jnp.sum(raw * raw, -1, keepdims=True) + 1e-06)
    unit = raw * inverse
    return unit, unit.astype(BF), inverse


def ids_down(packed_ref):
    return across(packed_ref[ROWS:, :ROWS], jnp.ones((16, ROWS), BF))


def turn(image_ref):
    return image_ref[:ROWS, :].astype(F32).T.astype(BF)


def pair(image_unit, ids, text_ref, scale, bias):
    logits = (
        scale
        * lax.dot_general(
            image_unit, text_ref[:ROWS, :], (((1,), (1,)), ((), ())), preferred_element_type=F32
        )
        + bias
    )
    match = ids == text_ref[ROWS:, :ROWS].astype(F32)[0:1, :]
    weight = 1.0 / (1.0 + jnp.exp(jnp.where(match, logits, -logits)))
    return jnp.where(match, -weight, weight).astype(BF)


def across(left, right):
    return lax.dot_general(left, right, (((0,), (0,)), ((), ())), preferred_element_type=F32)


def back(image_grad, unit, inverse):
    inner = jnp.sum(image_grad * unit, -1, keepdims=True)
    return ((image_grad - unit * inner) * inverse).astype(BF)


def own_kernel(
    grp_ref, scale_ref, bias_ref, shard0_ref, shard1_ref, shard2_ref, shard3_ref, image_ref, text_ref, weight_ref, raw_grad_ref, grad_ref, sems
):
    grp = grp_ref[0]
    loads = []
    for flip, shard_ref in enumerate((shard0_ref, shard1_ref, shard2_ref, shard3_ref)):
        rows = pl.ds(pl.multiple_of((grp ^ flip) * SHARD, 32), SHARD)
        loads.append(pltpu.make_async_copy(shard_ref, weight_ref.at[rows, :], sems.at[flip]))
        loads[-1].start()
    for load in loads:
        load.wait()
    scale, bias = scale_ref[0], bias_ref[0]
    unit, image_unit, inverse = project(image_ref, weight_ref)
    near = pair(image_unit, ids_down(image_ref), text_ref, scale, bias)
    grad_ref[...] = across(near, image_unit)
    image_grad = scale * jnp.dot(near, text_ref[:ROWS, :], preferred_element_type=F32)
    raw_grad_ref[...] = back(image_grad, unit, inverse)


def next_kernel(
    scale_ref, bias_ref, weight_ref, image0_ref, raw_grad0_ref, image1_ref, text_ref, text1_ref, grad0_ref, part_ref, grad_ref,
    turned_ref, raw_grads_ref
):
    turned_ref[:, :ROWS] = turn(image0_ref)
    turned_ref[:, ROWS:] = turn(image1_ref)
    raw_grads_ref[:ROWS, :] = raw_grad0_ref[...]
    scale, bias = scale_ref[0], bias_ref[0]
    unit, image_unit, inverse = project(image1_ref, weight_ref)
    ids = ids_down(image1_ref)
    near = pair(image_unit, ids, text_ref, scale, bias)
    far = pair(image_unit, ids, text1_ref, scale, bias)
    grad_ref[...] = grad0_ref[...] + across(near, image_unit)
    image_grad = scale * (
        jnp.dot(near, text_ref[:ROWS, :], preferred_element_type=F32)
        + jnp.dot(far, text1_ref[:ROWS, :], preferred_element_type=F32)
    )
    raw_grads_ref[ROWS:, :] = back(image_grad, unit, inverse)
    part_ref[...] = jnp.dot(turned_ref[...], raw_grads_ref[...], preferred_element_type=F32)


def load_quarters(core, part_ref, rows_ref, sems):
    loads = []
    for half in range(2):
        at = pl.multiple_of((2 * half + core) * SHARD, 32)
        loads.append(
            pltpu.make_async_copy(
                part_ref.at[pl.ds(at, SHARD), :],
                rows_ref.at[pl.ds(half * SHARD, SHARD), :],
                sems.at[half],
            )
        )
    for load in loads:
        load.start()
    return loads


def add_quarters(core, turned_ref, raw_grad, rows_ref, loads, out_ref):
    for half in range(2):
        at = pl.multiple_of((2 * half + core) * SHARD, 32)
        rows = pl.ds(half * SHARD, SHARD)
        term = jnp.dot(turned_ref[pl.ds(at, SHARD), :], raw_grad, preferred_element_type=F32)
        loads[half].wait()
        out_ref[rows, :] = (rows_ref[rows, :] + term).astype(BF)


def last_kernel(
    grp_ref, scale_ref, bias_ref, weight_ref, image_ref, text1_ref, part_ref,
    send_ref, turned_ref, raw_grad_ref, image_unit_ref, far_ref, rows_ref, sems
):
    core = 1 - grp_ref[0] % 2
    loads = load_quarters(core, part_ref, rows_ref, sems)
    scale, bias = scale_ref[0], bias_ref[0]
    turned_ref[...] = turn(image_ref)
    unit, image_unit, inverse = project(image_ref, weight_ref)
    image_unit_ref[...] = image_unit
    far = pair(image_unit, ids_down(image_ref), text1_ref, scale, bias)
    far_ref[...] = far
    image_grad = scale * jnp.dot(far, text1_ref[:ROWS, :], preferred_element_type=F32)
    raw_grad = back(image_grad, unit, inverse)
    raw_grad_ref[...] = raw_grad
    add_quarters(core, turned_ref, raw_grad, rows_ref, loads, send_ref)


def keep_kernel(grp_ref, turned_ref, raw_grad_ref, image_unit_ref, far_ref, part_ref, keep_ref, back_ref, rows_ref, sems):
    core = grp_ref[0] % 2
    loads = load_quarters(core, part_ref, rows_ref, sems)
    add_quarters(core, turned_ref, raw_grad_ref[...], rows_ref, loads, keep_ref)
    back_ref[...] = across(far_ref[...], image_unit_ref[...]).astype(BF)


def finish_kernel(odd_ref, scale_ref, bias_ref, image_unit2_ref, image2_ref, text_ref, grad_ref, even_back_ref, odd_back_ref, out_ref):
    image_unit2 = image_unit2_ref[...]
    back = jnp.where(odd_ref[0] == 1, odd_back_ref[1], even_back_ref[1]).astype(F32)
    near2 = pair(image_unit2, ids_down(image2_ref), text_ref, scale_ref[0], bias_ref[0])
    out_ref[...] = scale_ref[0] * (grad_ref[...] + across(near2, image_unit2) + back)


def shape(rows, columns, dtype):
    return jax.ShapeDtypeStruct((rows, columns), dtype)


def on_device(feats, proj_weight, text_embed, row_ids, logit_scale, logit_bias):
    packed = shape(PACKED, D, BF)
    grp = lax.axis_index("grp").astype(jnp.int32).reshape(1)
    numbers = (logit_scale, logit_bias)
    flops = 2 * ROWS * D * D
    anywhere = pl.BlockSpec(memory_space=pl.ANY)
    scratch = [pltpu.VMEM((2 * SHARD, D), F32), pltpu.SemaphoreType.DMA((2,))]
    ids = row_ids.reshape(1, ROWS)
    image0 = call(pack_kernel, [packed], [VMEM] * 2, ROWS)(feats, ids)[0]
    image0, text_embed = lax.optimization_barrier((image0, text_embed))
    text0 = call(text_kernel, [packed], [VMEM] * 2, ROWS)(text_embed, ids)[0]
    shard1 = move(proj_weight, CORES)
    shard2 = move(proj_weight, swap_x((1, 3)))
    image1 = shift(image0, -1)
    shard2, text0 = lax.optimization_barrier((shard2, text0))
    shard3 = move(shard2, CORES)
    text1 = shift(text0, 1)
    image2 = shift(image1, -1)
    weight, raw_grad0, grad = call(
        own_kernel, [shape(D, D, BF), shape(ROWS, D, BF), shape(ROWS, D, F32)], [SMEM] * 3 + [anywhere] * 4 + [VMEM] * 2, flops,
        [pltpu.SemaphoreType.DMA((4,))],
    )(grp, *numbers, proj_weight, shard1, shard2, shard3, image0, text0)
    part, grad = call(
        next_kernel,
        [shape(D, D, F32), shape(ROWS, D, F32)],
        [SMEM] * 2 + [VMEM] * 7,
        4 * flops,
        [pltpu.VMEM((D, 2 * ROWS), BF), pltpu.VMEM((2 * ROWS, D), BF)],
    )(*numbers, weight, image0, raw_grad0, image1, text0, text1, grad)
    send, turned, raw_grad2, image_unit2, far = call(
        last_kernel,
        [shape(2 * SHARD, D, BF), shape(D, ROWS, BF), shape(ROWS, D, BF), shape(ROWS, D, BF), shape(ROWS, ROWS, BF)],
        [SMEM] * 3 + [VMEM] * 3 + [anywhere],
        2 * flops,
        scratch,
    )(grp, *numbers, weight, image2, text1, part)
    keep, term = call(
        keep_kernel,
        [shape(2 * SHARD, D, BF), shape(ROWS, D, BF)],
        [SMEM] + [VMEM] * 4 + [anywhere],
        flops,
        scratch,
    )(grp, turned, raw_grad2, image_unit2, far, part)
    even = lax.all_gather(term, AXIS, axis_index_groups=EVEN)
    odd = lax.all_gather(term, AXIS, axis_index_groups=ODD)
    halves = (keep.astype(F32) + move(send, CORES).astype(F32)).astype(BF)
    mine = total(exchange(halves.reshape(8, SUB, D), FIRST))
    tiles = mine.reshape(SUB, 9, 128).transpose(1, 0, 2).reshape(SUB * 9, 128)
    tiles = jnp.pad(tiles, ((0, 768 - SUB * 9), (0, 0))).reshape(16, 48, 128)
    done = total(exchange(tiles, FAR))
    done = (done.astype(F32) + move(done, swap_x((2, 2))).astype(F32)).astype(BF)
    done = spread(done, FAR).reshape(768, 128)[:704]
    done = spread(done, NEAR)[:, : SUB * 9]
    weight_grad = done.reshape(4, 9, SUB, 128).transpose(0, 2, 1, 3).reshape(SHARD, D).astype(F32)
    text_grad = call(finish_kernel, [shape(ROWS, D, F32)], [SMEM] * 3 + [VMEM] * 6, flops)(
        (lax.axis_index("blk") % 2).astype(jnp.int32).reshape(1), *numbers, image_unit2, image2, text0, grad, even, odd
    )[0]
    return (weight_grad, text_grad)


def solution(mesh):
    return jax.shard_map(
        on_device,
        mesh=mesh,
        in_specs=(P(AXIS, None), P("grp", None), P(AXIS, None), P(AXIS), P(), P()),
        out_specs=(P("grp", None), P(AXIS, None)),
        check_vma=False,
    )
```

```python
import jax
import jax.numpy as jnp
from jax import lax
from jax.experimental import pallas as pl
from jax.experimental.pallas import tpu as pltpu
from jax.sharding import PartitionSpec as P

BF = jnp.bfloat16
F32 = jnp.float32
ROWS = 256
D = 1152
SHARD = D // 4
SUB = SHARD // 4
PACKED = ROWS + 16
N = 512
AXIS = ("blk", "grp")
VMEM = pl.BlockSpec(memory_space=pltpu.VMEM)
SMEM = pl.BlockSpec(memory_space=pltpu.SMEM)


def coordinates(device):
    blk, grp = divmod(device, 4)
    return blk // 16, (blk // 8) % 2 * 2 + grp // 2, blk % 8, grp % 2


def device_at(z, x, y, core):
    return ((z % 8 * 2 + x % 4 // 2) * 8 + y % 8) * 4 + x % 2 * 2 + core


def swap_x(flips):
    moves = []
    for device in range(N):
        z, x, y, core = coordinates(device)
        moves.append((device_at(z, x ^ flips[core], y, core), device))
    return moves


def grouped(same, place):
    groups = {}
    for device in range(N):
        z, x, y, core = coordinates(device)
        key = (z + core) % 8, (x + core) % 4, (y + core) % 8, x % 2, core
        groups.setdefault(same(*key), []).append((place(*key), device))
    return [[device for _, device in sorted(group)] for group in groups.values()]


FIRST = grouped(lambda z, x, y, xl, core: (z // 2, x // 2, y // 2, core), lambda z, x, y, xl, core: (xl, z % 2, y % 2))
NEAR = grouped(lambda z, x, y, xl, core: (z // 2, x, y // 2, core), lambda z, x, y, xl, core: (z % 2, y % 2))
FAR = grouped(lambda z, x, y, xl, core: (z % 2, x, y % 2, core), lambda z, x, y, xl, core: (z // 2, y // 2))
CORES = [(i ^ 1, i) for i in range(N)]


def shift(block, distance):
    return lax.ppermute(block, AXIS, [((i - 4 * distance) % N, i) for i in range(N)])


def move(block, moves):
    return lax.ppermute(block, AXIS, moves)


def exchange(chunks, groups):
    return lax.all_to_all(chunks, AXIS, 0, 0, axis_index_groups=groups, tiled=True)


def spread(chunk, groups):
    return exchange(jnp.broadcast_to(chunk[None], (len(groups[0]),) + chunk.shape), groups)


def total(chunks):
    return jnp.sum(chunks.astype(F32), 0).astype(BF)


def call(kernel, outs, specs, flops, scratch=()):
    def run(*args):
        moved = sum(a.size * a.dtype.itemsize for a in args) + sum(
            o.size * o.dtype.itemsize for o in outs
        )
        return pl.pallas_call(
            kernel,
            out_shape=outs,
            in_specs=specs,
            out_specs=[VMEM] * len(outs),
            scratch_shapes=scratch,
            compiler_params=pltpu.CompilerParams(vmem_limit_bytes=20 * 1024 * 1024),
            cost_estimate=pl.CostEstimate(flops=flops, bytes_accessed=moved, transcendentals=0),
        )(*args)

    return run


def top_row(ids_ref):
    first = lax.broadcasted_iota(jnp.int32, (16, ROWS), 0) == 0
    ids = jnp.broadcast_to(ids_ref[...].astype(F32), (16, ROWS))
    return jnp.where(first, ids, 0.0).astype(BF)


def put_ids(ids_ref, out_ref):
    out_ref[ROWS:, :ROWS] = top_row(ids_ref)
    out_ref[ROWS:, ROWS:] = jnp.zeros((16, D - ROWS), BF)


def prepare_kernel(feats_ref, text_ref, ids_ref, image_ref, out_ref, rows_ref, sems):
    loads = [
        pltpu.make_async_copy(text_ref, rows_ref, sems.at[0]),
        pltpu.make_async_copy(feats_ref, image_ref.at[pl.ds(0, ROWS), :], sems.at[1]),
    ]
    for load in loads:
        load.start()
    put_ids(ids_ref, image_ref)
    put_ids(ids_ref, out_ref)
    loads[0].wait()
    rows = rows_ref[...].astype(F32)
    inverse = 1.0 / jnp.sqrt(jnp.sum(rows * rows, -1, keepdims=True) + 1e-06)
    out_ref[:ROWS, :] = (rows * inverse).astype(BF)
    loads[1].wait()


def project(image_ref, weight_ref):
    raw = jnp.dot(image_ref[:ROWS, :], weight_ref[...], preferred_element_type=F32)
    inverse = 1.0 / jnp.sqrt(jnp.sum(raw * raw, -1, keepdims=True) + 1e-06)
    unit = raw * inverse
    return unit, unit.astype(BF), inverse


def ids_down(packed_ref):
    return across(packed_ref[ROWS:, :ROWS], jnp.ones((16, ROWS), BF))


def turn(image_ref):
    return image_ref[:ROWS, :].astype(F32).T.astype(BF)


def pair(image_unit, ids, text_ref, scale, bias):
    logits = (
        scale
        * lax.dot_general(
            image_unit, text_ref[:ROWS, :], (((1,), (1,)), ((), ())), preferred_element_type=F32
        )
        + bias
    )
    match = ids == text_ref[ROWS:, :ROWS].astype(F32)[0:1, :]
    weight = 1.0 / (1.0 + jnp.exp(jnp.where(match, logits, -logits)))
    return jnp.where(match, -weight, weight).astype(BF)


def across(left, right):
    return lax.dot_general(left, right, (((0,), (0,)), ((), ())), preferred_element_type=F32)


def back(image_grad, unit, inverse):
    inner = jnp.sum(image_grad * unit, -1, keepdims=True)
    return ((image_grad - unit * inner) * inverse).astype(BF)


def own_kernel(
    grp_ref, scale_ref, bias_ref, shard0_ref, shard1_ref, shard2_ref, shard3_ref, image_ref, text_ref, weight_ref, raw_grad_ref, grad_ref, sems
):
    grp = grp_ref[0]
    loads = []
    for flip, shard_ref in enumerate((shard0_ref, shard1_ref, shard2_ref, shard3_ref)):
        rows = pl.ds(pl.multiple_of((grp ^ flip) * SHARD, 32), SHARD)
        loads.append(pltpu.make_async_copy(shard_ref, weight_ref.at[rows, :], sems.at[flip]))
        loads[-1].start()
    for load in loads:
        load.wait()
    scale, bias = scale_ref[0], bias_ref[0]
    unit, image_unit, inverse = project(image_ref, weight_ref)
    near = pair(image_unit, ids_down(image_ref), text_ref, scale, bias)
    grad_ref[...] = across(near, image_unit)
    image_grad = scale * jnp.dot(near, text_ref[:ROWS, :], preferred_element_type=F32)
    raw_grad_ref[...] = back(image_grad, unit, inverse)


def next_kernel(
    scale_ref, bias_ref, weight_ref, image0_ref, raw_grad0_ref, image1_ref, text_ref, text1_ref, grad0_ref, part_ref, grad_ref,
    turned_ref, raw_grads_ref
):
    turned_ref[:, :ROWS] = turn(image0_ref)
    turned_ref[:, ROWS:] = turn(image1_ref)
    raw_grads_ref[:ROWS, :] = raw_grad0_ref[...]
    scale, bias = scale_ref[0], bias_ref[0]
    unit, image_unit, inverse = project(image1_ref, weight_ref)
    ids = ids_down(image1_ref)
    near = pair(image_unit, ids, text_ref, scale, bias)
    far = pair(image_unit, ids, text1_ref, scale, bias)
    grad_ref[...] = grad0_ref[...] + across(near, image_unit)
    image_grad = scale * (
        jnp.dot(near, text_ref[:ROWS, :], preferred_element_type=F32)
        + jnp.dot(far, text1_ref[:ROWS, :], preferred_element_type=F32)
    )
    raw_grads_ref[ROWS:, :] = back(image_grad, unit, inverse)
    part_ref[...] = jnp.dot(turned_ref[...], raw_grads_ref[...], preferred_element_type=F32)


def load_quarters(core, part_ref, rows_ref, sems):
    loads = []
    for half in range(2):
        at = pl.multiple_of((2 * half + core) * SHARD, 32)
        loads.append(
            pltpu.make_async_copy(
                part_ref.at[pl.ds(at, SHARD), :],
                rows_ref.at[pl.ds(half * SHARD, SHARD), :],
                sems.at[half],
            )
        )
    for load in loads:
        load.start()
    return loads


def add_quarters(core, turned_ref, raw_grad, rows_ref, loads, out_ref):
    for half in range(2):
        at = pl.multiple_of((2 * half + core) * SHARD, 32)
        rows = pl.ds(half * SHARD, SHARD)
        term = jnp.dot(turned_ref[pl.ds(at, SHARD), :], raw_grad, preferred_element_type=F32)
        loads[half].wait()
        out_ref[rows, :] = (rows_ref[rows, :] + term).astype(BF)


def last_kernel(
    grp_ref, scale_ref, bias_ref, weight_ref, image_ref, text1_ref, part_ref,
    send_ref, turned_ref, raw_grad_ref, image_unit_ref, far_ref, rows_ref, sems
):
    core = 1 - grp_ref[0] % 2
    loads = load_quarters(core, part_ref, rows_ref, sems)
    scale, bias = scale_ref[0], bias_ref[0]
    turned_ref[...] = turn(image_ref)
    unit, image_unit, inverse = project(image_ref, weight_ref)
    image_unit_ref[...] = image_unit
    far = pair(image_unit, ids_down(image_ref), text1_ref, scale, bias)
    far_ref[...] = far
    image_grad = scale * jnp.dot(far, text1_ref[:ROWS, :], preferred_element_type=F32)
    raw_grad = back(image_grad, unit, inverse)
    raw_grad_ref[...] = raw_grad
    add_quarters(core, turned_ref, raw_grad, rows_ref, loads, send_ref)


def keep_kernel(grp_ref, turned_ref, raw_grad_ref, image_unit_ref, far_ref, part_ref, keep_ref, back_ref, rows_ref, sems):
    core = grp_ref[0] % 2
    loads = load_quarters(core, part_ref, rows_ref, sems)
    add_quarters(core, turned_ref, raw_grad_ref[...], rows_ref, loads, keep_ref)
    back_ref[...] = across(far_ref[...], image_unit_ref[...]).astype(BF)


def finish_kernel(scale_ref, bias_ref, image_unit2_ref, image2_ref, text_ref, grad_ref, back_ref, out_ref):
    image_unit2 = image_unit2_ref[...]
    near2 = pair(image_unit2, ids_down(image2_ref), text_ref, scale_ref[0], bias_ref[0])
    out_ref[...] = scale_ref[0] * (grad_ref[...] + across(near2, image_unit2) + back_ref[...].astype(F32))


def shape(rows, columns, dtype):
    return jax.ShapeDtypeStruct((rows, columns), dtype)


def on_device(feats, proj_weight, text_embed, row_ids, logit_scale, logit_bias):
    packed = shape(PACKED, D, BF)
    grp = lax.axis_index("grp").astype(jnp.int32).reshape(1)
    numbers = (logit_scale, logit_bias)
    flops = 2 * ROWS * D * D
    anywhere = pl.BlockSpec(memory_space=pl.ANY)
    hbm = pl.BlockSpec(memory_space=pltpu.HBM)
    scratch = [pltpu.VMEM((2 * SHARD, D), F32), pltpu.SemaphoreType.DMA((2,))]
    ids = row_ids.reshape(1, ROWS)
    image0, text0 = call(
        prepare_kernel,
        [packed] * 2,
        [hbm] * 2 + [VMEM],
        ROWS,
        [pltpu.VMEM((ROWS, D), BF), pltpu.SemaphoreType.DMA((2,))],
    )(feats, text_embed, ids)
    proj_weight, image0, text0 = lax.optimization_barrier((proj_weight, image0, text0))
    image1 = shift(image0, -1)
    text1 = shift(text0, 1)
    shard2 = move(proj_weight, swap_x((1, 3)))
    shard1 = move(proj_weight, CORES)
    shard3 = move(lax.optimization_barrier((shard2, text1, image1))[0], CORES)
    image2 = shift(image1, -1)
    weight, raw_grad0, grad = call(
        own_kernel, [shape(D, D, BF), shape(ROWS, D, BF), shape(ROWS, D, F32)], [SMEM] * 3 + [hbm] * 4 + [VMEM] * 2, flops,
        [pltpu.SemaphoreType.DMA((4,))],
    )(grp, *numbers, proj_weight, shard1, shard2, shard3, image0, text0)
    part, grad = call(
        next_kernel,
        [shape(D, D, F32), shape(ROWS, D, F32)],
        [SMEM] * 2 + [VMEM] * 7,
        4 * flops,
        [pltpu.VMEM((D, 2 * ROWS), BF), pltpu.VMEM((2 * ROWS, D), BF)],
    )(*numbers, weight, image0, raw_grad0, image1, text0, text1, grad)
    send, turned, raw_grad2, image_unit2, far = call(
        last_kernel,
        [shape(2 * SHARD, D, BF), shape(D, ROWS, BF), shape(ROWS, D, BF), shape(ROWS, D, BF), shape(ROWS, ROWS, BF)],
        [SMEM] * 3 + [VMEM] * 3 + [anywhere],
        2 * flops,
        scratch,
    )(grp, *numbers, weight, image2, text1, part)
    keep, term = call(
        keep_kernel,
        [shape(2 * SHARD, D, BF), shape(ROWS, D, BF)],
        [SMEM] + [VMEM] * 4 + [anywhere],
        flops,
        scratch,
    )(grp, turned, raw_grad2, image_unit2, far, part)
    halves = (keep.astype(F32) + move(send, CORES).astype(F32)).astype(BF)
    mine = total(exchange(halves.reshape(8, SUB, D), FIRST))
    tiles = mine.reshape(SUB, 9, 128).transpose(1, 0, 2).reshape(SUB * 9, 128)
    tiles = jnp.pad(tiles, ((0, 768 - SUB * 9), (0, 0))).reshape(16, 48, 128)
    done = total(exchange(tiles, FAR))
    done = (done.astype(F32) + move(done, swap_x((2, 2))).astype(F32)).astype(BF)
    done, term = lax.optimization_barrier((done, term))
    term = shift(term, -1)
    done = spread(done, FAR).reshape(768, 128)[:704]
    done, term = lax.optimization_barrier((done, term))
    done = spread(done, NEAR)[:, : SUB * 9]
    weight_grad = done.reshape(4, 9, SUB, 128).transpose(0, 2, 1, 3).reshape(SHARD, D).astype(F32)
    text_grad = call(finish_kernel, [shape(ROWS, D, F32)], [SMEM] * 2 + [VMEM] * 5, flops)(
        *numbers, image_unit2, image2, text0, grad, term
    )[0]
    return (weight_grad, text_grad)


def solution(mesh):
    return jax.shard_map(
        on_device,
        mesh=mesh,
        in_specs=(P(AXIS, None), P("grp", None), P(AXIS, None), P(AXIS), P(), P()),
        out_specs=(P("grp", None), P(AXIS, None)),
        check_vma=False,
    )
```

```python
import jax
import jax.numpy as jnp
from jax import lax
from jax.experimental import pallas as pl
from jax.experimental.pallas import tpu as pltpu
from jax.sharding import PartitionSpec as P

BF = jnp.bfloat16
F32 = jnp.float32
ROWS = 256
D = 1152
SHARD = D // 4
SUB = SHARD // 4
PACKED = ROWS + 16
BAND = SUB + 8
N = 512
AXIS = ("blk", "grp")
VMEM = pl.BlockSpec(memory_space=pltpu.VMEM)
SMEM = pl.BlockSpec(memory_space=pltpu.SMEM)


def coordinates(device):
    blk, grp = divmod(device, 4)
    return blk // 16, (blk // 8) % 2 * 2 + grp // 2, blk % 8, grp % 2


def device_at(z, x, y, core):
    return ((z % 8 * 2 + x % 4 // 2) * 8 + y % 8) * 4 + x % 2 * 2 + core


def swap_x(flips):
    moves = []
    for device in range(N):
        z, x, y, core = coordinates(device)
        moves.append((device_at(z, x ^ flips[core], y, core), device))
    return moves


def grouped(same, place):
    groups = {}
    for device in range(N):
        z, x, y, core = coordinates(device)
        key = (z + core) % 8, (x + core) % 4, (y + core) % 8, x % 2, core
        groups.setdefault(same(*key), []).append((place(*key), device))
    return [[device for _, device in sorted(group)] for group in groups.values()]


FIRST = grouped(lambda z, x, y, xl, core: (z // 2, x // 2, y // 2, core), lambda z, x, y, xl, core: (xl, z % 2, y % 2))
NEAR = grouped(lambda z, x, y, xl, core: (z // 2, x, y // 2, core), lambda z, x, y, xl, core: (z % 2, y % 2))
FAR = grouped(lambda z, x, y, xl, core: (z % 2, x, y % 2, core), lambda z, x, y, xl, core: (z // 2, y // 2))
CORES = [(i ^ 1, i) for i in range(N)]


def shift(block, distance):
    return lax.ppermute(block, AXIS, [((i - 4 * distance) % N, i) for i in range(N)])


def move(block, moves):
    return lax.ppermute(block, AXIS, moves)


def exchange(chunks, groups):
    return lax.all_to_all(chunks, AXIS, 0, 0, axis_index_groups=groups, tiled=True)


def spread(chunk, groups):
    return exchange(jnp.broadcast_to(chunk[None], (len(groups[0]),) + chunk.shape), groups)


def total(chunks):
    return jnp.sum(chunks.astype(F32), 0).astype(BF)


def call(kernel, outs, specs, flops, scratch=()):
    def run(*args):
        moved = sum(a.size * a.dtype.itemsize for a in args) + sum(
            o.size * o.dtype.itemsize for o in outs
        )
        return pl.pallas_call(
            kernel,
            out_shape=outs,
            in_specs=specs,
            out_specs=[VMEM] * len(outs),
            scratch_shapes=scratch,
            compiler_params=pltpu.CompilerParams(vmem_limit_bytes=20 * 1024 * 1024),
            cost_estimate=pl.CostEstimate(flops=flops, bytes_accessed=moved, transcendentals=0),
        )(*args)

    return run


def top_row(ids_ref):
    first = lax.broadcasted_iota(jnp.int32, (16, ROWS), 0) == 0
    ids = jnp.broadcast_to(ids_ref[...].astype(F32), (16, ROWS))
    return jnp.where(first, ids, 0.0).astype(BF)


def put_ids(ids_ref, out_ref):
    out_ref[ROWS:, :ROWS] = top_row(ids_ref)
    out_ref[ROWS:, ROWS:] = jnp.zeros((16, D - ROWS), BF)


def prepare_kernel(feats_ref, text_ref, ids_ref, image_ref, out_ref, rows_ref, sems):
    loads = [
        pltpu.make_async_copy(text_ref, rows_ref, sems.at[0]),
        pltpu.make_async_copy(feats_ref, image_ref.at[pl.ds(0, ROWS), :], sems.at[1]),
    ]
    for load in loads:
        load.start()
    put_ids(ids_ref, image_ref)
    put_ids(ids_ref, out_ref)
    loads[0].wait()
    rows = rows_ref[...].astype(F32)
    inverse = 1.0 / jnp.sqrt(jnp.sum(rows * rows, -1, keepdims=True) + 1e-06)
    out_ref[:ROWS, :] = (rows * inverse).astype(BF)
    loads[1].wait()


def project(image_ref, weight_ref):
    raw = jnp.dot(image_ref[:ROWS, :], weight_ref[...], preferred_element_type=F32)
    inverse = 1.0 / jnp.sqrt(jnp.sum(raw * raw, -1, keepdims=True) + 1e-06)
    unit = raw * inverse
    return unit, unit.astype(BF), inverse


def ids_down(packed_ref):
    return across(packed_ref[ROWS:, :ROWS], jnp.ones((16, ROWS), BF))


def turn(image_ref):
    return image_ref[:ROWS, :].astype(F32).T.astype(BF)


def pair(image_unit, ids, text_ref, scale, bias):
    logits = (
        scale
        * lax.dot_general(
            image_unit, text_ref[:ROWS, :], (((1,), (1,)), ((), ())), preferred_element_type=F32
        )
        + bias
    )
    match = ids == text_ref[ROWS:, :ROWS].astype(F32)[0:1, :]
    weight = 1.0 / (1.0 + jnp.exp(jnp.where(match, logits, -logits)))
    return jnp.where(match, -weight, weight).astype(BF)


def across(left, right):
    return lax.dot_general(left, right, (((0,), (0,)), ((), ())), preferred_element_type=F32)


def back(image_grad, unit, inverse):
    inner = jnp.sum(image_grad * unit, -1, keepdims=True)
    return ((image_grad - unit * inner) * inverse).astype(BF)


def own_kernel(
    grp_ref, scale_ref, bias_ref, shard0_ref, shard1_ref, shard2_ref, shard3_ref, image_ref, text_ref, weight_ref, raw_grad_ref, grad_ref, sems
):
    grp = grp_ref[0]
    loads = []
    for flip, shard_ref in enumerate((shard0_ref, shard1_ref, shard2_ref, shard3_ref)):
        rows = pl.ds(pl.multiple_of((grp ^ flip) * SHARD, 32), SHARD)
        loads.append(pltpu.make_async_copy(shard_ref, weight_ref.at[rows, :], sems.at[flip]))
        loads[-1].start()
    for load in loads:
        load.wait()
    scale, bias = scale_ref[0], bias_ref[0]
    unit, image_unit, inverse = project(image_ref, weight_ref)
    near = pair(image_unit, ids_down(image_ref), text_ref, scale, bias)
    grad_ref[...] = across(near, image_unit)
    image_grad = scale * jnp.dot(near, text_ref[:ROWS, :], preferred_element_type=F32)
    raw_grad_ref[...] = back(image_grad, unit, inverse)


def next_kernel(
    scale_ref, bias_ref, weight_ref, image0_ref, raw_grad0_ref, image1_ref, text_ref, text1_ref, grad0_ref, part_ref, grad_ref,
    turned_ref, raw_grads_ref
):
    turned_ref[:, :ROWS] = turn(image0_ref)
    turned_ref[:, ROWS:] = turn(image1_ref)
    raw_grads_ref[:ROWS, :] = raw_grad0_ref[...]
    scale, bias = scale_ref[0], bias_ref[0]
    unit, image_unit, inverse = project(image1_ref, weight_ref)
    ids = ids_down(image1_ref)
    near = pair(image_unit, ids, text_ref, scale, bias)
    far = pair(image_unit, ids, text1_ref, scale, bias)
    grad_ref[...] = grad0_ref[...] + across(near, image_unit)
    image_grad = scale * (
        jnp.dot(near, text_ref[:ROWS, :], preferred_element_type=F32)
        + jnp.dot(far, text1_ref[:ROWS, :], preferred_element_type=F32)
    )
    raw_grads_ref[ROWS:, :] = back(image_grad, unit, inverse)
    part_ref[...] = jnp.dot(turned_ref[...], raw_grads_ref[...], preferred_element_type=F32)


def load_quarters(core, part_ref, rows_ref, sems):
    loads = []
    for half in range(2):
        at = pl.multiple_of((2 * half + core) * SHARD, 32)
        loads.append(
            pltpu.make_async_copy(
                part_ref.at[pl.ds(at, SHARD), :],
                rows_ref.at[pl.ds(half * SHARD, SHARD), :],
                sems.at[half],
            )
        )
    for load in loads:
        load.start()
    return loads


def add_quarters(core, turned_ref, raw_grad, rows_ref, loads, out_ref):
    for half in range(2):
        at = pl.multiple_of((2 * half + core) * SHARD, 32)
        rows = pl.ds(half * SHARD, SHARD)
        term = jnp.dot(turned_ref[pl.ds(at, SHARD), :], raw_grad, preferred_element_type=F32)
        loads[half].wait()
        out_ref[rows, :] = (rows_ref[rows, :] + term).astype(BF)


def last_kernel(
    grp_ref, scale_ref, bias_ref, weight_ref, image_ref, text1_ref, part_ref,
    send_ref, turned_ref, raw_grad_ref, image_unit_ref, far_ref, rows_ref, sems
):
    core = 1 - grp_ref[0] % 2
    loads = load_quarters(core, part_ref, rows_ref, sems)
    scale, bias = scale_ref[0], bias_ref[0]
    turned_ref[...] = turn(image_ref)
    unit, image_unit, inverse = project(image_ref, weight_ref)
    image_unit_ref[...] = image_unit
    far = pair(image_unit, ids_down(image_ref), text1_ref, scale, bias)
    far_ref[...] = far
    image_grad = scale * jnp.dot(far, text1_ref[:ROWS, :], preferred_element_type=F32)
    raw_grad = back(image_grad, unit, inverse)
    raw_grad_ref[...] = raw_grad
    add_quarters(core, turned_ref, raw_grad, rows_ref, loads, send_ref)


def keep_kernel(grp_ref, turned_ref, raw_grad_ref, image_unit_ref, far_ref, part_ref, keep_ref, back_ref, rows_ref, sems):
    core = grp_ref[0] % 2
    loads = load_quarters(core, part_ref, rows_ref, sems)
    add_quarters(core, turned_ref, raw_grad_ref[...], rows_ref, loads, keep_ref)
    back_ref[...] = across(far_ref[...], image_unit_ref[...]).astype(BF)


def finish_kernel(scale_ref, bias_ref, image_unit2_ref, image2_ref, text_ref, grad_ref, back_ref, out_ref):
    image_unit2 = image_unit2_ref[...]
    near2 = pair(image_unit2, ids_down(image2_ref), text_ref, scale_ref[0], bias_ref[0])
    out_ref[...] = scale_ref[0] * (grad_ref[...] + across(near2, image_unit2) + back_ref[...].astype(F32))


def pack_kernel(chunks_ref, out_ref):
    rows = chunks_ref[0].astype(F32)
    for chunk in range(1, 8):
        rows = rows + chunks_ref[chunk].astype(F32)
    for band in range(9):
        tile = jnp.concatenate([rows[:, band * 128 : (band + 1) * 128], jnp.zeros((8, 128), F32)], 0)
        out_ref[band * BAND : (band + 1) * BAND, :] = tile.astype(BF)
    out_ref[9 * BAND :, :] = jnp.zeros((768 - 9 * BAND, 128), BF)


def unpack_kernel(tiles_ref, out_ref):
    for chunk in range(4):
        for band in range(9):
            tile = tiles_ref[chunk, band * BAND : (band + 1) * BAND, :].astype(F32)
            out_ref[chunk * SUB : (chunk + 1) * SUB, band * 128 : (band + 1) * 128] = tile[:SUB]


def shape(rows, columns, dtype):
    return jax.ShapeDtypeStruct((rows, columns), dtype)


def on_device(feats, proj_weight, text_embed, row_ids, logit_scale, logit_bias):
    packed = shape(PACKED, D, BF)
    grp = lax.axis_index("grp").astype(jnp.int32).reshape(1)
    numbers = (logit_scale, logit_bias)
    flops = 2 * ROWS * D * D
    anywhere = pl.BlockSpec(memory_space=pl.ANY)
    hbm = pl.BlockSpec(memory_space=pltpu.HBM)
    scratch = [pltpu.VMEM((2 * SHARD, D), F32), pltpu.SemaphoreType.DMA((2,))]
    ids = row_ids.reshape(1, ROWS)
    image0, text0 = call(
        prepare_kernel,
        [packed] * 2,
        [hbm] * 2 + [VMEM],
        ROWS,
        [pltpu.VMEM((ROWS, D), BF), pltpu.SemaphoreType.DMA((2,))],
    )(feats, text_embed, ids)
    image1 = shift(image0, -1)
    text1 = shift(text0, 1)
    shard2 = move(proj_weight, swap_x((1, 3)))
    shard1 = move(proj_weight, CORES)
    shard3 = move(lax.optimization_barrier((shard2, text1))[0], CORES)
    image2 = shift(image1, -1)
    weight, raw_grad0, grad = call(
        own_kernel, [shape(D, D, BF), shape(ROWS, D, BF), shape(ROWS, D, F32)], [SMEM] * 3 + [hbm] * 4 + [VMEM] * 2, flops,
        [pltpu.SemaphoreType.DMA((4,))],
    )(grp, *numbers, proj_weight, shard1, shard2, shard3, image0, text0)
    part, grad = call(
        next_kernel,
        [shape(D, D, F32), shape(ROWS, D, F32)],
        [SMEM] * 2 + [VMEM] * 7,
        4 * flops,
        [pltpu.VMEM((D, 2 * ROWS), BF), pltpu.VMEM((2 * ROWS, D), BF)],
    )(*numbers, weight, image0, raw_grad0, image1, text0, text1, grad)
    send, turned, raw_grad2, image_unit2, far = call(
        last_kernel,
        [shape(2 * SHARD, D, BF), shape(D, ROWS, BF), shape(ROWS, D, BF), shape(ROWS, D, BF), shape(ROWS, ROWS, BF)],
        [SMEM] * 3 + [VMEM] * 3 + [anywhere],
        2 * flops,
        scratch,
    )(grp, *numbers, weight, image2, text1, part)
    keep, term = call(
        keep_kernel,
        [shape(2 * SHARD, D, BF), shape(ROWS, D, BF)],
        [SMEM] + [VMEM] * 4 + [anywhere],
        flops,
        scratch,
    )(grp, turned, raw_grad2, image_unit2, far, part)
    halves = (keep.astype(F32) + move(send, CORES).astype(F32)).astype(BF)
    mine = exchange(halves.reshape(8, SUB, D), FIRST)
    tiles = call(pack_kernel, [shape(768, 128, BF)], [VMEM], ROWS)(mine)[0]
    tiles, term = lax.optimization_barrier((tiles, term))
    tiles = tiles.reshape(16, 48, 128)
    term = shift(term, -1)
    done = total(exchange(tiles, FAR))
    done = (done.astype(F32) + move(done, swap_x((2, 2))).astype(F32)).astype(BF)
    done = spread(done, FAR).reshape(768, 128)[: 9 * BAND]
    done, term = lax.optimization_barrier((done, term))
    done = spread(done, NEAR)
    weight_grad = call(unpack_kernel, [shape(SHARD, D, F32)], [VMEM], ROWS)(done)[0]
    text_grad = call(finish_kernel, [shape(ROWS, D, F32)], [SMEM] * 2 + [VMEM] * 5, flops)(
        *numbers, image_unit2, image2, text0, grad, term
    )[0]
    return (weight_grad, text_grad)


def solution(mesh):
    return jax.shard_map(
        on_device,
        mesh=mesh,
        in_specs=(P(AXIS, None), P("grp", None), P(AXIS, None), P(AXIS), P(), P()),
        out_specs=(P("grp", None), P(AXIS, None)),
        check_vma=False,
    )
```

```python
import jax
import jax.numpy as jnp
from jax import lax
from jax.experimental import pallas as pl
from jax.experimental.pallas import tpu as pltpu
from jax.sharding import PartitionSpec as P

BF = jnp.bfloat16
F32 = jnp.float32
ROWS = 256
D = 1152
SHARD = D // 4
SUB = SHARD // 4
PACKED = ROWS + 16
BAND = SUB + 8
N = 512
AXIS = ("blk", "grp")
VMEM = pl.BlockSpec(memory_space=pltpu.VMEM)
SMEM = pl.BlockSpec(memory_space=pltpu.SMEM)


def coordinates(device):
    blk, grp = divmod(device, 4)
    return blk // 16, (blk // 8) % 2 * 2 + grp // 2, blk % 8, grp % 2


def device_at(z, x, y, core):
    return ((z % 8 * 2 + x % 4 // 2) * 8 + y % 8) * 4 + x % 2 * 2 + core


def swap_x(flips):
    moves = []
    for device in range(N):
        z, x, y, core = coordinates(device)
        moves.append((device_at(z, x ^ flips[core], y, core), device))
    return moves


def grouped(same, place):
    groups = {}
    for device in range(N):
        z, x, y, core = coordinates(device)
        key = (z + core) % 8, (x + core) % 4, (y + core) % 8, x % 2, core
        groups.setdefault(same(*key), []).append((place(*key), device))
    return [[device for _, device in sorted(group)] for group in groups.values()]


FIRST = grouped(lambda z, x, y, xl, core: (z // 2, x // 2, y // 2, core), lambda z, x, y, xl, core: (xl, z % 2, y % 2))
NEAR = grouped(lambda z, x, y, xl, core: (z // 2, x, y // 2, core), lambda z, x, y, xl, core: (z % 2, y % 2))
FAR = grouped(lambda z, x, y, xl, core: (z % 2, x, y % 2, core), lambda z, x, y, xl, core: (z // 2, y // 2))
CORES = [(i ^ 1, i) for i in range(N)]


def shift(block, distance):
    return lax.ppermute(block, AXIS, [((i - 4 * distance) % N, i) for i in range(N)])


def move(block, moves):
    return lax.ppermute(block, AXIS, moves)


def exchange(chunks, groups):
    return lax.all_to_all(chunks, AXIS, 0, 0, axis_index_groups=groups, tiled=True)


def spread(chunk, groups):
    return exchange(jnp.broadcast_to(chunk[None], (len(groups[0]),) + chunk.shape), groups)


def total(chunks):
    return jnp.sum(chunks.astype(F32), 0).astype(BF)


def call(kernel, outs, specs, flops, scratch=()):
    def run(*args):
        moved = sum(a.size * a.dtype.itemsize for a in args) + sum(
            o.size * o.dtype.itemsize for o in outs
        )
        return pl.pallas_call(
            kernel,
            out_shape=outs,
            in_specs=specs,
            out_specs=[VMEM] * len(outs),
            scratch_shapes=scratch,
            compiler_params=pltpu.CompilerParams(vmem_limit_bytes=20 * 1024 * 1024),
            cost_estimate=pl.CostEstimate(flops=flops, bytes_accessed=moved, transcendentals=0),
        )(*args)

    return run


def top_row(ids_ref):
    first = lax.broadcasted_iota(jnp.int32, (16, ROWS), 0) == 0
    ids = jnp.broadcast_to(ids_ref[...].astype(F32), (16, ROWS))
    return jnp.where(first, ids, 0.0).astype(BF)


def put_ids(ids_ref, out_ref):
    out_ref[ROWS:, :ROWS] = top_row(ids_ref)
    out_ref[ROWS:, ROWS:] = jnp.zeros((16, D - ROWS), BF)


def prepare_kernel(feats_ref, text_ref, ids_ref, image_ref, out_ref, rows_ref, sems):
    loads = [
        pltpu.make_async_copy(text_ref, rows_ref, sems.at[0]),
        pltpu.make_async_copy(feats_ref, image_ref.at[pl.ds(0, ROWS), :], sems.at[1]),
    ]
    for load in loads:
        load.start()
    put_ids(ids_ref, image_ref)
    put_ids(ids_ref, out_ref)
    loads[0].wait()
    rows = rows_ref[...].astype(F32)
    inverse = 1.0 / jnp.sqrt(jnp.sum(rows * rows, -1, keepdims=True) + 1e-06)
    out_ref[:ROWS, :] = (rows * inverse).astype(BF)
    loads[1].wait()


def project(image_ref, weight_ref):
    raw = jnp.dot(image_ref[:ROWS, :], weight_ref[...], preferred_element_type=F32)
    inverse = 1.0 / jnp.sqrt(jnp.sum(raw * raw, -1, keepdims=True) + 1e-06)
    unit = raw * inverse
    return unit, unit.astype(BF), inverse


def ids_down(packed_ref):
    return across(packed_ref[ROWS:, :ROWS], jnp.ones((16, ROWS), BF))


def turn(image_ref):
    return image_ref[:ROWS, :].astype(F32).T.astype(BF)


def pair(image_unit, ids, text_ref, scale, bias):
    logits = (
        scale
        * lax.dot_general(
            image_unit, text_ref[:ROWS, :], (((1,), (1,)), ((), ())), preferred_element_type=F32
        )
        + bias
    )
    match = ids == text_ref[ROWS:, :ROWS].astype(F32)[0:1, :]
    weight = 1.0 / (1.0 + jnp.exp(jnp.where(match, logits, -logits)))
    return jnp.where(match, -weight, weight).astype(BF)


def across(left, right):
    return lax.dot_general(left, right, (((0,), (0,)), ((), ())), preferred_element_type=F32)


def back(image_grad, unit, inverse):
    inner = jnp.sum(image_grad * unit, -1, keepdims=True)
    return ((image_grad - unit * inner) * inverse).astype(BF)


def own_kernel(
    grp_ref, scale_ref, bias_ref, shard0_ref, shard1_ref, shard2_ref, shard3_ref, image_ref, text_ref, weight_ref, raw_grad_ref, grad_ref, sems
):
    grp = grp_ref[0]
    loads = []
    for flip, shard_ref in enumerate((shard0_ref, shard1_ref, shard2_ref, shard3_ref)):
        rows = pl.ds(pl.multiple_of((grp ^ flip) * SHARD, 32), SHARD)
        loads.append(pltpu.make_async_copy(shard_ref, weight_ref.at[rows, :], sems.at[flip]))
        loads[-1].start()
    for load in loads:
        load.wait()
    scale, bias = scale_ref[0], bias_ref[0]
    unit, image_unit, inverse = project(image_ref, weight_ref)
    near = pair(image_unit, ids_down(image_ref), text_ref, scale, bias)
    grad_ref[...] = across(near, image_unit)
    image_grad = scale * jnp.dot(near, text_ref[:ROWS, :], preferred_element_type=F32)
    raw_grad_ref[...] = back(image_grad, unit, inverse)


def next_kernel(
    scale_ref, bias_ref, weight_ref, image0_ref, raw_grad0_ref, image1_ref, text_ref, text1_ref, grad0_ref, part_ref, grad_ref,
    turned_ref, raw_grads_ref
):
    turned_ref[:, :ROWS] = turn(image0_ref)
    turned_ref[:, ROWS:] = turn(image1_ref)
    raw_grads_ref[:ROWS, :] = raw_grad0_ref[...]
    scale, bias = scale_ref[0], bias_ref[0]
    unit, image_unit, inverse = project(image1_ref, weight_ref)
    ids = ids_down(image1_ref)
    near = pair(image_unit, ids, text_ref, scale, bias)
    far = pair(image_unit, ids, text1_ref, scale, bias)
    grad_ref[...] = grad0_ref[...] + across(near, image_unit)
    image_grad = scale * (
        jnp.dot(near, text_ref[:ROWS, :], preferred_element_type=F32)
        + jnp.dot(far, text1_ref[:ROWS, :], preferred_element_type=F32)
    )
    raw_grads_ref[ROWS:, :] = back(image_grad, unit, inverse)
    part_ref[...] = jnp.dot(turned_ref[...], raw_grads_ref[...], preferred_element_type=F32)


def load_quarters(core, part_ref, rows_ref, sems):
    loads = []
    for half in range(2):
        at = pl.multiple_of((2 * half + core) * SHARD, 32)
        loads.append(
            pltpu.make_async_copy(
                part_ref.at[pl.ds(at, SHARD), :],
                rows_ref.at[pl.ds(half * SHARD, SHARD), :],
                sems.at[half],
            )
        )
    for load in loads:
        load.start()
    return loads


def add_quarters(core, turned_ref, raw_grad, rows_ref, loads, out_ref):
    for half in range(2):
        at = pl.multiple_of((2 * half + core) * SHARD, 32)
        rows = pl.ds(half * SHARD, SHARD)
        term = jnp.dot(turned_ref[pl.ds(at, SHARD), :], raw_grad, preferred_element_type=F32)
        loads[half].wait()
        out_ref[rows, :] = (rows_ref[rows, :] + term).astype(BF)


def last_kernel(
    grp_ref, scale_ref, bias_ref, weight_ref, image_ref, text1_ref, part_ref,
    send_ref, turned_ref, raw_grad_ref, image_unit_ref, far_ref, rows_ref, sems
):
    core = 1 - grp_ref[0] % 2
    loads = load_quarters(core, part_ref, rows_ref, sems)
    scale, bias = scale_ref[0], bias_ref[0]
    turned_ref[...] = turn(image_ref)
    unit, image_unit, inverse = project(image_ref, weight_ref)
    image_unit_ref[...] = image_unit
    far = pair(image_unit, ids_down(image_ref), text1_ref, scale, bias)
    far_ref[...] = far
    image_grad = scale * jnp.dot(far, text1_ref[:ROWS, :], preferred_element_type=F32)
    raw_grad = back(image_grad, unit, inverse)
    raw_grad_ref[...] = raw_grad
    add_quarters(core, turned_ref, raw_grad, rows_ref, loads, send_ref)


def keep_kernel(grp_ref, turned_ref, raw_grad_ref, image_unit_ref, far_ref, part_ref, keep_ref, back_ref, rows_ref, sems):
    core = grp_ref[0] % 2
    loads = load_quarters(core, part_ref, rows_ref, sems)
    add_quarters(core, turned_ref, raw_grad_ref[...], rows_ref, loads, keep_ref)
    back_ref[...] = across(far_ref[...], image_unit_ref[...]).astype(BF)


def finish_kernel(scale_ref, bias_ref, image_unit2_ref, image2_ref, text_ref, grad_ref, back_ref, out_ref):
    image_unit2 = image_unit2_ref[...]
    near2 = pair(image_unit2, ids_down(image2_ref), text_ref, scale_ref[0], bias_ref[0])
    out_ref[...] = scale_ref[0] * (grad_ref[...] + across(near2, image_unit2) + back_ref[...].astype(F32))


def pack_kernel(chunks_ref, out_ref):
    rows = chunks_ref[0].astype(F32)
    for chunk in range(1, 8):
        rows = rows + chunks_ref[chunk].astype(F32)
    for band in range(9):
        tile = jnp.concatenate([rows[:, band * 128 : (band + 1) * 128], jnp.zeros((8, 128), F32)], 0)
        out_ref[band * BAND : (band + 1) * BAND, :] = tile.astype(BF)
    out_ref[9 * BAND :, :] = jnp.zeros((768 - 9 * BAND, 128), BF)


def unpack_kernel(tiles_ref, out_ref):
    for chunk in range(4):
        for band in range(9):
            tile = tiles_ref[chunk, band * BAND : (band + 1) * BAND, :].astype(F32)
            out_ref[chunk * SUB : (chunk + 1) * SUB, band * 128 : (band + 1) * 128] = tile[:SUB]


def shape(rows, columns, dtype):
    return jax.ShapeDtypeStruct((rows, columns), dtype)


def on_device(feats, proj_weight, text_embed, row_ids, logit_scale, logit_bias):
    packed = shape(PACKED, D, BF)
    grp = lax.axis_index("grp").astype(jnp.int32).reshape(1)
    numbers = (logit_scale, logit_bias)
    flops = 2 * ROWS * D * D
    anywhere = pl.BlockSpec(memory_space=pl.ANY)
    hbm = pl.BlockSpec(memory_space=pltpu.HBM)
    scratch = [pltpu.VMEM((2 * SHARD, D), F32), pltpu.SemaphoreType.DMA((2,))]
    ids = row_ids.reshape(1, ROWS)
    image0, text0 = call(
        prepare_kernel,
        [packed] * 2,
        [hbm] * 2 + [VMEM],
        ROWS,
        [pltpu.VMEM((ROWS, D), BF), pltpu.SemaphoreType.DMA((2,))],
    )(feats, text_embed, ids)
    image1 = shift(image0, -1)
    text1 = shift(text0, 1)
    shard2 = move(proj_weight, swap_x((1, 3)))
    shard1 = move(proj_weight, CORES)
    shard3 = move(lax.optimization_barrier((shard2, text1))[0], CORES)
    image2 = shift(image1, -1)
    weight, raw_grad0, grad = call(
        own_kernel, [shape(D, D, BF), shape(ROWS, D, BF), shape(ROWS, D, F32)], [SMEM] * 3 + [hbm] * 4 + [VMEM] * 2, flops,
        [pltpu.SemaphoreType.DMA((4,))],
    )(grp, *numbers, proj_weight, shard1, shard2, shard3, image0, text0)
    part, grad = call(
        next_kernel,
        [shape(D, D, F32), shape(ROWS, D, F32)],
        [SMEM] * 2 + [VMEM] * 7,
        4 * flops,
        [pltpu.VMEM((D, 2 * ROWS), BF), pltpu.VMEM((2 * ROWS, D), BF)],
    )(*numbers, weight, image0, raw_grad0, image1, text0, text1, grad)
    send, turned, raw_grad2, image_unit2, far = call(
        last_kernel,
        [shape(2 * SHARD, D, BF), shape(D, ROWS, BF), shape(ROWS, D, BF), shape(ROWS, D, BF), shape(ROWS, ROWS, BF)],
        [SMEM] * 3 + [VMEM] * 3 + [anywhere],
        2 * flops,
        scratch,
    )(grp, *numbers, weight, image2, text1, part)
    keep, term = call(
        keep_kernel,
        [shape(2 * SHARD, D, BF), shape(ROWS, D, BF)],
        [SMEM] + [VMEM] * 4 + [anywhere],
        flops,
        scratch,
    )(grp, turned, raw_grad2, image_unit2, far, part)
    halves = (keep.astype(F32) + move(send, CORES).astype(F32)).astype(BF)
    mine = exchange(halves.reshape(8, SUB, D), FIRST)
    tiles = call(pack_kernel, [shape(768, 128, BF)], [VMEM], ROWS)(mine)[0]
    tiles = tiles.reshape(16, 48, 128)
    term = shift(term, -1)
    done = total(exchange(tiles, FAR))
    done, term = lax.optimization_barrier((done, term))
    done = (done.astype(F32) + move(done, swap_x((2, 2))).astype(F32)).astype(BF)
    done = spread(done, FAR).reshape(768, 128)[: 9 * BAND]
    done = spread(done, NEAR)
    weight_grad = call(unpack_kernel, [shape(SHARD, D, F32)], [VMEM], ROWS)(done)[0]
    text_grad = call(finish_kernel, [shape(ROWS, D, F32)], [SMEM] * 2 + [VMEM] * 5, flops)(
        *numbers, image_unit2, image2, text0, grad, term
    )[0]
    return (weight_grad, text_grad)


def solution(mesh):
    return jax.shard_map(
        on_device,
        mesh=mesh,
        in_specs=(P(AXIS, None), P("grp", None), P(AXIS, None), P(AXIS), P(), P()),
        out_specs=(P("grp", None), P(AXIS, None)),
        check_vma=False,
    )
```

```python
import jax
import jax.numpy as jnp
from jax import lax
from jax.experimental import pallas as pl
from jax.experimental.pallas import tpu as pltpu
from jax.sharding import PartitionSpec as P

BF = jnp.bfloat16
F32 = jnp.float32
ROWS = 256
D = 1152
SHARD = D // 4
SUB = SHARD // 4
PACKED = ROWS + 16
BAND = SUB + 8
N = 512
AXIS = ("blk", "grp")
VMEM = pl.BlockSpec(memory_space=pltpu.VMEM)
SMEM = pl.BlockSpec(memory_space=pltpu.SMEM)


def coordinates(device):
    blk, grp = divmod(device, 4)
    return blk // 16, (blk // 8) % 2 * 2 + grp // 2, blk % 8, grp % 2


def device_at(z, x, y, core):
    return ((z % 8 * 2 + x % 4 // 2) * 8 + y % 8) * 4 + x % 2 * 2 + core


def swap_x(flips):
    moves = []
    for device in range(N):
        z, x, y, core = coordinates(device)
        moves.append((device_at(z, x ^ flips[core], y, core), device))
    return moves


def grouped(same, place):
    groups = {}
    for device in range(N):
        z, x, y, core = coordinates(device)
        key = (z + core) % 8, (x + core) % 4, (y + core) % 8, x % 2, core
        groups.setdefault(same(*key), []).append((place(*key), device))
    return [[device for _, device in sorted(group)] for group in groups.values()]


FIRST = grouped(lambda z, x, y, xl, core: (z // 2, x // 2, y // 2, core), lambda z, x, y, xl, core: (xl, z % 2, y % 2))
NEAR = grouped(lambda z, x, y, xl, core: (z // 2, x, y // 2, core), lambda z, x, y, xl, core: (z % 2, y % 2))
FAR = grouped(lambda z, x, y, xl, core: (z % 2, x, y % 2, core), lambda z, x, y, xl, core: (z // 2, y // 2))
CORES = [(i ^ 1, i) for i in range(N)]


def shift(block, distance):
    return lax.ppermute(block, AXIS, [((i - 4 * distance) % N, i) for i in range(N)])


def move(block, moves):
    return lax.ppermute(block, AXIS, moves)


def exchange(chunks, groups):
    return lax.all_to_all(chunks, AXIS, 0, 0, axis_index_groups=groups, tiled=True)


def spread(chunk, groups):
    return exchange(jnp.broadcast_to(chunk[None], (len(groups[0]),) + chunk.shape), groups)


def total(chunks):
    return jnp.sum(chunks.astype(F32), 0).astype(BF)


def call(kernel, outs, specs, flops, scratch=(), vmem=20):
    def run(*args):
        moved = sum(a.size * a.dtype.itemsize for a in args) + sum(
            o.size * o.dtype.itemsize for o in outs
        )
        return pl.pallas_call(
            kernel,
            out_shape=outs,
            in_specs=specs,
            out_specs=[VMEM] * len(outs),
            scratch_shapes=scratch,
            compiler_params=pltpu.CompilerParams(vmem_limit_bytes=vmem * 1024 * 1024),
            cost_estimate=pl.CostEstimate(flops=flops, bytes_accessed=moved, transcendentals=0),
        )(*args)

    return run


def top_row(ids_ref):
    first = lax.broadcasted_iota(jnp.int32, (16, ROWS), 0) == 0
    ids = jnp.broadcast_to(ids_ref[...].astype(F32), (16, ROWS))
    return jnp.where(first, ids, 0.0).astype(BF)


def put_ids(ids_ref, out_ref):
    out_ref[ROWS:, :ROWS] = top_row(ids_ref)
    out_ref[ROWS:, ROWS:] = jnp.zeros((16, D - ROWS), BF)


def prepare_kernel(feats_ref, text_ref, ids_ref, image_ref, out_ref, rows_ref, sems):
    loads = [
        pltpu.make_async_copy(text_ref, rows_ref, sems.at[0]),
        pltpu.make_async_copy(feats_ref, image_ref.at[pl.ds(0, ROWS), :], sems.at[1]),
    ]
    for load in loads:
        load.start()
    put_ids(ids_ref, image_ref)
    put_ids(ids_ref, out_ref)
    loads[0].wait()
    rows = rows_ref[...].astype(F32)
    inverse = 1.0 / jnp.sqrt(jnp.sum(rows * rows, -1, keepdims=True) + 1e-06)
    out_ref[:ROWS, :] = (rows * inverse).astype(BF)
    loads[1].wait()


def project(image_ref, weight_ref):
    raw = jnp.dot(image_ref[:ROWS, :], weight_ref[...], preferred_element_type=F32)
    inverse = 1.0 / jnp.sqrt(jnp.sum(raw * raw, -1, keepdims=True) + 1e-06)
    unit = raw * inverse
    return unit, unit.astype(BF), inverse


def ids_down(packed_ref):
    return across(packed_ref[ROWS:, :ROWS], jnp.ones((16, ROWS), BF))


def turn(image_ref):
    return image_ref[:ROWS, :].astype(F32).T.astype(BF)


def pair(image_unit, ids, text_ref, scale, bias):
    logits = (
        scale
        * lax.dot_general(
            image_unit, text_ref[:ROWS, :], (((1,), (1,)), ((), ())), preferred_element_type=F32
        )
        + bias
    )
    match = ids == text_ref[ROWS:, :ROWS].astype(F32)[0:1, :]
    weight = 1.0 / (1.0 + jnp.exp(jnp.where(match, logits, -logits)))
    return jnp.where(match, -weight, weight).astype(BF)


def across(left, right):
    return lax.dot_general(left, right, (((0,), (0,)), ((), ())), preferred_element_type=F32)


def back(image_grad, unit, inverse):
    inner = jnp.sum(image_grad * unit, -1, keepdims=True)
    return ((image_grad - unit * inner) * inverse).astype(BF)


def own_kernel(
    grp_ref, scale_ref, bias_ref, shard0_ref, shard1_ref, shard2_ref, shard3_ref, image_ref, text_ref, weight_ref, raw_grad_ref, grad_ref, sems
):
    grp = grp_ref[0]
    loads = []
    for flip, shard_ref in enumerate((shard0_ref, shard1_ref, shard2_ref, shard3_ref)):
        rows = pl.ds(pl.multiple_of((grp ^ flip) * SHARD, 32), SHARD)
        loads.append(pltpu.make_async_copy(shard_ref, weight_ref.at[rows, :], sems.at[flip]))
        loads[-1].start()
    for load in loads:
        load.wait()
    scale, bias = scale_ref[0], bias_ref[0]
    unit, image_unit, inverse = project(image_ref, weight_ref)
    near = pair(image_unit, ids_down(image_ref), text_ref, scale, bias)
    grad_ref[...] = across(near, image_unit)
    image_grad = scale * jnp.dot(near, text_ref[:ROWS, :], preferred_element_type=F32)
    raw_grad_ref[...] = back(image_grad, unit, inverse)


def next_kernel(
    scale_ref, bias_ref, weight_ref, image0_ref, raw_grad0_ref, image1_ref, text_ref, text1_ref, grad0_ref, part_ref, grad_ref,
    turned_ref, raw_grads_ref
):
    turned_ref[:, :ROWS] = turn(image0_ref)
    turned_ref[:, ROWS:] = turn(image1_ref)
    raw_grads_ref[:ROWS, :] = raw_grad0_ref[...]
    scale, bias = scale_ref[0], bias_ref[0]
    unit, image_unit, inverse = project(image1_ref, weight_ref)
    ids = ids_down(image1_ref)
    near = pair(image_unit, ids, text_ref, scale, bias)
    far = pair(image_unit, ids, text1_ref, scale, bias)
    grad_ref[...] = grad0_ref[...] + across(near, image_unit)
    image_grad = scale * (
        jnp.dot(near, text_ref[:ROWS, :], preferred_element_type=F32)
        + jnp.dot(far, text1_ref[:ROWS, :], preferred_element_type=F32)
    )
    raw_grads_ref[ROWS:, :] = back(image_grad, unit, inverse)
    part_ref[...] = jnp.dot(turned_ref[...], raw_grads_ref[...], preferred_element_type=F32)


def load_quarters(core, part_ref, rows_ref, sems):
    loads = []
    for half in range(2):
        at = pl.multiple_of((2 * half + core) * SHARD, 32)
        loads.append(
            pltpu.make_async_copy(
                part_ref.at[pl.ds(at, SHARD), :],
                rows_ref.at[pl.ds(half * SHARD, SHARD), :],
                sems.at[half],
            )
        )
    for load in loads:
        load.start()
    return loads


def add_quarters(core, turned_ref, raw_grad, rows_ref, loads, out_ref):
    for half in range(2):
        at = pl.multiple_of((2 * half + core) * SHARD, 32)
        rows = pl.ds(half * SHARD, SHARD)
        term = jnp.dot(turned_ref[pl.ds(at, SHARD), :], raw_grad, preferred_element_type=F32)
        loads[half].wait()
        out_ref[rows, :] = (rows_ref[rows, :] + term).astype(BF)


def last_kernel(
    grp_ref, scale_ref, bias_ref, weight_ref, image_ref, text1_ref, part_ref,
    send_ref, turned_ref, raw_grad_ref, image_unit_ref, far_ref, rows_ref, sems
):
    core = 1 - grp_ref[0] % 2
    loads = load_quarters(core, part_ref, rows_ref, sems)
    scale, bias = scale_ref[0], bias_ref[0]
    turned_ref[...] = turn(image_ref)
    unit, image_unit, inverse = project(image_ref, weight_ref)
    image_unit_ref[...] = image_unit
    far = pair(image_unit, ids_down(image_ref), text1_ref, scale, bias)
    far_ref[...] = far
    image_grad = scale * jnp.dot(far, text1_ref[:ROWS, :], preferred_element_type=F32)
    raw_grad = back(image_grad, unit, inverse)
    raw_grad_ref[...] = raw_grad
    add_quarters(core, turned_ref, raw_grad, rows_ref, loads, send_ref)


def keep_kernel(grp_ref, turned_ref, raw_grad_ref, image_unit_ref, far_ref, part_ref, keep_ref, back_ref, rows_ref, sems):
    core = grp_ref[0] % 2
    loads = load_quarters(core, part_ref, rows_ref, sems)
    add_quarters(core, turned_ref, raw_grad_ref[...], rows_ref, loads, keep_ref)
    back_ref[...] = across(far_ref[...], image_unit_ref[...]).astype(BF)


def finish_kernel(scale_ref, bias_ref, image_unit2_ref, image2_ref, text_ref, grad_ref, back_ref, out_ref):
    image_unit2 = image_unit2_ref[...]
    near2 = pair(image_unit2, ids_down(image2_ref), text_ref, scale_ref[0], bias_ref[0])
    out_ref[...] = scale_ref[0] * (grad_ref[...] + across(near2, image_unit2) + back_ref[...].astype(F32))


def pack_kernel(chunks_ref, out_ref):
    rows = chunks_ref[0].astype(F32)
    for chunk in range(1, 8):
        rows = rows + chunks_ref[chunk].astype(F32)
    for band in range(9):
        tile = jnp.concatenate([rows[:, band * 128 : (band + 1) * 128], jnp.zeros((8, 128), F32)], 0)
        out_ref[band * BAND : (band + 1) * BAND, :] = tile.astype(BF)
    out_ref[9 * BAND :, :] = jnp.zeros((768 - 9 * BAND, 128), BF)


def unpack_kernel(tiles_ref, out_ref):
    for chunk in range(4):
        for band in range(9):
            tile = tiles_ref[chunk, band * BAND : (band + 1) * BAND, :].astype(F32)
            out_ref[chunk * SUB : (chunk + 1) * SUB, band * 128 : (band + 1) * 128] = tile[:SUB]


def shape(rows, columns, dtype):
    return jax.ShapeDtypeStruct((rows, columns), dtype)


def on_device(feats, proj_weight, text_embed, row_ids, logit_scale, logit_bias):
    packed = shape(PACKED, D, BF)
    grp = lax.axis_index("grp").astype(jnp.int32).reshape(1)
    numbers = (logit_scale, logit_bias)
    flops = 2 * ROWS * D * D
    anywhere = pl.BlockSpec(memory_space=pl.ANY)
    hbm = pl.BlockSpec(memory_space=pltpu.HBM)
    scratch = [pltpu.VMEM((2 * SHARD, D), F32), pltpu.SemaphoreType.DMA((2,))]
    ids = row_ids.reshape(1, ROWS)
    image0, text0 = call(
        prepare_kernel,
        [packed] * 2,
        [hbm] * 2 + [VMEM],
        ROWS,
        [pltpu.VMEM((ROWS, D), BF), pltpu.SemaphoreType.DMA((2,))],
        62,
    )(feats, text_embed, ids)
    image1 = shift(image0, -1)
    text1 = shift(text0, 1)
    shard2 = move(proj_weight, swap_x((1, 3)))
    shard1 = move(proj_weight, CORES)
    shard3 = move(lax.optimization_barrier((shard2, text1))[0], CORES)
    image2 = shift(image1, -1)
    weight, raw_grad0, grad = call(
        own_kernel, [shape(D, D, BF), shape(ROWS, D, BF), shape(ROWS, D, F32)], [SMEM] * 3 + [hbm] * 4 + [VMEM] * 2, flops,
        [pltpu.SemaphoreType.DMA((4,))],
    )(grp, *numbers, proj_weight, shard1, shard2, shard3, image0, text0)
    part, grad = call(
        next_kernel,
        [shape(D, D, F32), shape(ROWS, D, F32)],
        [SMEM] * 2 + [VMEM] * 7,
        4 * flops,
        [pltpu.VMEM((D, 2 * ROWS), BF), pltpu.VMEM((2 * ROWS, D), BF)],
    )(*numbers, weight, image0, raw_grad0, image1, text0, text1, grad)
    send, turned, raw_grad2, image_unit2, far = call(
        last_kernel,
        [shape(2 * SHARD, D, BF), shape(D, ROWS, BF), shape(ROWS, D, BF), shape(ROWS, D, BF), shape(ROWS, ROWS, BF)],
        [SMEM] * 3 + [VMEM] * 3 + [anywhere],
        2 * flops,
        scratch,
    )(grp, *numbers, weight, image2, text1, part)
    keep, term = call(
        keep_kernel,
        [shape(2 * SHARD, D, BF), shape(ROWS, D, BF)],
        [SMEM] + [VMEM] * 4 + [anywhere],
        flops,
        scratch,
    )(grp, turned, raw_grad2, image_unit2, far, part)
    halves = (keep.astype(F32) + move(send, CORES).astype(F32)).astype(BF)
    mine = exchange(halves.reshape(8, SUB, D), FIRST)
    tiles = call(pack_kernel, [shape(768, 128, BF)], [VMEM], ROWS)(mine)[0]
    tiles, term = lax.optimization_barrier((tiles, term))
    tiles = tiles.reshape(16, 48, 128)
    term = shift(term, -1)
    done = total(exchange(tiles, FAR))
    done = (done.astype(F32) + move(done, swap_x((2, 2))).astype(F32)).astype(BF)
    done = spread(done, FAR).reshape(768, 128)[: 9 * BAND]
    done, term = lax.optimization_barrier((done, term))
    done = spread(done, NEAR)
    weight_grad = call(unpack_kernel, [shape(SHARD, D, F32)], [VMEM], ROWS)(done)[0]
    text_grad = call(finish_kernel, [shape(ROWS, D, F32)], [SMEM] * 2 + [VMEM] * 5, flops)(
        *numbers, image_unit2, image2, text0, grad, term
    )[0]
    return (weight_grad, text_grad)


def solution(mesh):
    return jax.shard_map(
        on_device,
        mesh=mesh,
        in_specs=(P(AXIS, None), P("grp", None), P(AXIS, None), P(AXIS), P(), P()),
        out_specs=(P("grp", None), P(AXIS, None)),
        check_vma=False,
    )
```

```python
import jax
import jax.numpy as jnp
from jax import lax
from jax.experimental import pallas as pl
from jax.experimental.pallas import tpu as pltpu
from jax.sharding import PartitionSpec as P

BF = jnp.bfloat16
F32 = jnp.float32
ROWS = 256
D = 1152
SHARD = D // 4
SUB = SHARD // 4
PACKED = ROWS + 16
BAND = SUB + 8
N = 512
AXIS = ("blk", "grp")
VMEM = pl.BlockSpec(memory_space=pltpu.VMEM)
SMEM = pl.BlockSpec(memory_space=pltpu.SMEM)


def coordinates(device):
    blk, grp = divmod(device, 4)
    return blk // 16, (blk // 8) % 2 * 2 + grp // 2, blk % 8, grp % 2


def device_at(z, x, y, core):
    return ((z % 8 * 2 + x % 4 // 2) * 8 + y % 8) * 4 + x % 2 * 2 + core


def swap_x(flips):
    moves = []
    for device in range(N):
        z, x, y, core = coordinates(device)
        moves.append((device_at(z, x ^ flips[core], y, core), device))
    return moves


def grouped(same, place):
    groups = {}
    for device in range(N):
        z, x, y, core = coordinates(device)
        key = (z + core) % 8, (x + core) % 4, (y + core) % 8, x % 2, core
        groups.setdefault(same(*key), []).append((place(*key), device))
    return [[device for _, device in sorted(group)] for group in groups.values()]


FIRST = grouped(lambda z, x, y, xl, core: (z // 2, x // 2, y // 2, core), lambda z, x, y, xl, core: (xl, z % 2, y % 2))
NEAR = grouped(lambda z, x, y, xl, core: (z // 2, x, y // 2, core), lambda z, x, y, xl, core: (z % 2, y % 2))
FAR = grouped(lambda z, x, y, xl, core: (z % 2, x, y % 2, core), lambda z, x, y, xl, core: (z // 2, y // 2))
CORES = [(i ^ 1, i) for i in range(N)]


def shift(block, distance):
    return lax.ppermute(block, AXIS, [((i - 4 * distance) % N, i) for i in range(N)])


def move(block, moves):
    return lax.ppermute(block, AXIS, moves)


def exchange(chunks, groups):
    return lax.all_to_all(chunks, AXIS, 0, 0, axis_index_groups=groups, tiled=True)


def spread(chunk, groups):
    return exchange(jnp.broadcast_to(chunk[None], (len(groups[0]),) + chunk.shape), groups)


def total(chunks):
    return jnp.sum(chunks.astype(F32), 0).astype(BF)


def call(kernel, outs, specs, flops, scratch=(), vmem=20):
    def run(*args):
        moved = sum(a.size * a.dtype.itemsize for a in args) + sum(
            o.size * o.dtype.itemsize for o in outs
        )
        return pl.pallas_call(
            kernel,
            out_shape=outs,
            in_specs=specs,
            out_specs=[VMEM] * len(outs),
            scratch_shapes=scratch,
            compiler_params=pltpu.CompilerParams(vmem_limit_bytes=vmem * 1024 * 1024),
            cost_estimate=pl.CostEstimate(flops=flops, bytes_accessed=moved, transcendentals=0),
        )(*args)

    return run


def top_row(ids_ref):
    first = lax.broadcasted_iota(jnp.int32, (16, ROWS), 0) == 0
    ids = jnp.broadcast_to(ids_ref[...].astype(F32), (16, ROWS))
    return jnp.where(first, ids, 0.0).astype(BF)


def put_ids(ids_ref, out_ref):
    out_ref[ROWS:, :ROWS] = top_row(ids_ref)
    out_ref[ROWS:, ROWS:] = jnp.zeros((16, D - ROWS), BF)


def prepare_kernel(feats_ref, text_ref, ids_ref, image_ref, out_ref, rows_ref, sems):
    loads = [
        pltpu.make_async_copy(text_ref, rows_ref, sems.at[0]),
        pltpu.make_async_copy(feats_ref, image_ref.at[pl.ds(0, ROWS), :], sems.at[1]),
    ]
    for load in loads:
        load.start()
    put_ids(ids_ref, image_ref)
    put_ids(ids_ref, out_ref)
    loads[0].wait()
    rows = rows_ref[...].astype(F32)
    inverse = 1.0 / jnp.sqrt(jnp.sum(rows * rows, -1, keepdims=True) + 1e-06)
    out_ref[:ROWS, :] = (rows * inverse).astype(BF)
    loads[1].wait()


def project(image_ref, weight_ref):
    raw = jnp.dot(image_ref[:ROWS, :], weight_ref[...], preferred_element_type=F32)
    inverse = 1.0 / jnp.sqrt(jnp.sum(raw * raw, -1, keepdims=True) + 1e-06)
    unit = raw * inverse
    return unit, unit.astype(BF), inverse


def ids_down(packed_ref):
    return across(packed_ref[ROWS:, :ROWS], jnp.ones((16, ROWS), BF))


def turn(image_ref):
    return image_ref[:ROWS, :].astype(F32).T.astype(BF)


def pair(image_unit, ids, text_ref, scale, bias):
    logits = (
        scale
        * lax.dot_general(
            image_unit, text_ref[:ROWS, :], (((1,), (1,)), ((), ())), preferred_element_type=F32
        )
        + bias
    )
    match = ids == text_ref[ROWS:, :ROWS].astype(F32)[0:1, :]
    weight = 1.0 / (1.0 + jnp.exp(jnp.where(match, logits, -logits)))
    return jnp.where(match, -weight, weight).astype(BF)


def across(left, right):
    return lax.dot_general(left, right, (((0,), (0,)), ((), ())), preferred_element_type=F32)


def back(image_grad, unit, inverse):
    inner = jnp.sum(image_grad * unit, -1, keepdims=True)
    return ((image_grad - unit * inner) * inverse).astype(BF)


def own_kernel(
    grp_ref, scale_ref, bias_ref, shard0_ref, shard1_ref, shard2_ref, shard3_ref, image_ref, text_ref, weight_ref, raw_grad_ref, grad_ref, sems
):
    grp = grp_ref[0]
    loads = []
    for flip, shard_ref in enumerate((shard0_ref, shard1_ref, shard2_ref, shard3_ref)):
        rows = pl.ds(pl.multiple_of((grp ^ flip) * SHARD, 32), SHARD)
        loads.append(pltpu.make_async_copy(shard_ref, weight_ref.at[rows, :], sems.at[flip]))
        loads[-1].start()
    for load in loads:
        load.wait()
    scale, bias = scale_ref[0], bias_ref[0]
    unit, image_unit, inverse = project(image_ref, weight_ref)
    near = pair(image_unit, ids_down(image_ref), text_ref, scale, bias)
    grad_ref[...] = across(near, image_unit)
    image_grad = scale * jnp.dot(near, text_ref[:ROWS, :], preferred_element_type=F32)
    raw_grad_ref[...] = back(image_grad, unit, inverse)


def next_kernel(
    scale_ref, bias_ref, weight_ref, image0_ref, raw_grad0_ref, image1_ref, text_ref, text1_ref, grad0_ref, part_ref, grad_ref,
    turned_ref, raw_grads_ref
):
    turned_ref[:, :ROWS] = turn(image0_ref)
    turned_ref[:, ROWS:] = turn(image1_ref)
    raw_grads_ref[:ROWS, :] = raw_grad0_ref[...]
    scale, bias = scale_ref[0], bias_ref[0]
    unit, image_unit, inverse = project(image1_ref, weight_ref)
    ids = ids_down(image1_ref)
    near = pair(image_unit, ids, text_ref, scale, bias)
    far = pair(image_unit, ids, text1_ref, scale, bias)
    grad_ref[...] = grad0_ref[...] + across(near, image_unit)
    image_grad = scale * (
        jnp.dot(near, text_ref[:ROWS, :], preferred_element_type=F32)
        + jnp.dot(far, text1_ref[:ROWS, :], preferred_element_type=F32)
    )
    raw_grads_ref[ROWS:, :] = back(image_grad, unit, inverse)
    part_ref[...] = jnp.dot(turned_ref[...], raw_grads_ref[...], preferred_element_type=F32)


def load_quarters(core, part_ref, rows_ref, sems):
    loads = []
    for half in range(2):
        at = pl.multiple_of((2 * half + core) * SHARD, 32)
        loads.append(
            pltpu.make_async_copy(
                part_ref.at[pl.ds(at, SHARD), :],
                rows_ref.at[pl.ds(half * SHARD, SHARD), :],
                sems.at[half],
            )
        )
    for load in loads:
        load.start()
    return loads


def add_quarters(core, turned_ref, raw_grad, rows_ref, loads, out_ref):
    for half in range(2):
        at = pl.multiple_of((2 * half + core) * SHARD, 32)
        rows = pl.ds(half * SHARD, SHARD)
        term = jnp.dot(turned_ref[pl.ds(at, SHARD), :], raw_grad, preferred_element_type=F32)
        loads[half].wait()
        out_ref[rows, :] = (rows_ref[rows, :] + term).astype(BF)


def last_kernel(
    grp_ref, scale_ref, bias_ref, weight_ref, image_ref, text1_ref, part_ref,
    send_ref, turned_ref, raw_grad_ref, image_unit_ref, far_ref, rows_ref, sems
):
    core = 1 - grp_ref[0] % 2
    loads = load_quarters(core, part_ref, rows_ref, sems)
    scale, bias = scale_ref[0], bias_ref[0]
    turned_ref[...] = turn(image_ref)
    unit, image_unit, inverse = project(image_ref, weight_ref)
    image_unit_ref[...] = image_unit
    far = pair(image_unit, ids_down(image_ref), text1_ref, scale, bias)
    far_ref[...] = far
    image_grad = scale * jnp.dot(far, text1_ref[:ROWS, :], preferred_element_type=F32)
    raw_grad = back(image_grad, unit, inverse)
    raw_grad_ref[...] = raw_grad
    add_quarters(core, turned_ref, raw_grad, rows_ref, loads, send_ref)


def keep_kernel(grp_ref, turned_ref, raw_grad_ref, image_unit_ref, far_ref, part_ref, keep_ref, back_ref, rows_ref, sems):
    core = grp_ref[0] % 2
    loads = load_quarters(core, part_ref, rows_ref, sems)
    add_quarters(core, turned_ref, raw_grad_ref[...], rows_ref, loads, keep_ref)
    back_ref[:ROWS, :] = across(far_ref[...], image_unit_ref[...]).astype(BF)
    back_ref[ROWS:, :] = jnp.zeros((16, D), BF)


def finish_kernel(scale_ref, bias_ref, image_unit2_ref, image2_ref, text_ref, grad_ref, back_ref, out_ref):
    image_unit2 = image_unit2_ref[...]
    near2 = pair(image_unit2, ids_down(image2_ref), text_ref, scale_ref[0], bias_ref[0])
    out_ref[...] = scale_ref[0] * (grad_ref[...] + across(near2, image_unit2) + back_ref[:ROWS, :].astype(F32))


def pack_kernel(chunks_ref, out_ref):
    rows = chunks_ref[0].astype(F32)
    for chunk in range(1, 8):
        rows = rows + chunks_ref[chunk].astype(F32)
    for band in range(9):
        tile = jnp.concatenate([rows[:, band * 128 : (band + 1) * 128], jnp.zeros((8, 128), F32)], 0)
        out_ref[band * BAND : (band + 1) * BAND, :] = tile.astype(BF)
    out_ref[9 * BAND :, :] = jnp.zeros((768 - 9 * BAND, 128), BF)


def unpack_kernel(tiles_ref, out_ref):
    for chunk in range(4):
        for band in range(9):
            tile = tiles_ref[chunk, band * BAND : (band + 1) * BAND, :].astype(F32)
            out_ref[chunk * SUB : (chunk + 1) * SUB, band * 128 : (band + 1) * 128] = tile[:SUB]


def shape(rows, columns, dtype):
    return jax.ShapeDtypeStruct((rows, columns), dtype)


def on_device(feats, proj_weight, text_embed, row_ids, logit_scale, logit_bias):
    packed = shape(PACKED, D, BF)
    grp = lax.axis_index("grp").astype(jnp.int32).reshape(1)
    numbers = (logit_scale, logit_bias)
    flops = 2 * ROWS * D * D
    anywhere = pl.BlockSpec(memory_space=pl.ANY)
    hbm = pl.BlockSpec(memory_space=pltpu.HBM)
    scratch = [pltpu.VMEM((2 * SHARD, D), F32), pltpu.SemaphoreType.DMA((2,))]
    ids = row_ids.reshape(1, ROWS)
    image0, text0 = call(
        prepare_kernel,
        [packed] * 2,
        [hbm] * 2 + [VMEM],
        ROWS,
        [pltpu.VMEM((ROWS, D), BF), pltpu.SemaphoreType.DMA((2,))],
        62,
    )(feats, text_embed, ids)
    image1 = shift(image0, -1)
    text1 = shift(text0, 1)
    shard2 = move(proj_weight, swap_x((1, 3)))
    shard1 = move(proj_weight, CORES)
    shard3 = move(lax.optimization_barrier((shard2, text1))[0], CORES)
    image2 = shift(image1, -1)
    weight, raw_grad0, grad = call(
        own_kernel, [shape(D, D, BF), shape(ROWS, D, BF), shape(ROWS, D, F32)], [SMEM] * 3 + [hbm] * 4 + [VMEM] * 2, flops,
        [pltpu.SemaphoreType.DMA((4,))],
    )(grp, *numbers, proj_weight, shard1, shard2, shard3, image0, text0)
    part, grad = call(
        next_kernel,
        [shape(D, D, F32), shape(ROWS, D, F32)],
        [SMEM] * 2 + [VMEM] * 7,
        4 * flops,
        [pltpu.VMEM((D, 2 * ROWS), BF), pltpu.VMEM((2 * ROWS, D), BF)],
    )(*numbers, weight, image0, raw_grad0, image1, text0, text1, grad)
    send, turned, raw_grad2, image_unit2, far = call(
        last_kernel,
        [shape(2 * SHARD, D, BF), shape(D, ROWS, BF), shape(ROWS, D, BF), shape(ROWS, D, BF), shape(ROWS, ROWS, BF)],
        [SMEM] * 3 + [VMEM] * 3 + [anywhere],
        2 * flops,
        scratch,
    )(grp, *numbers, weight, image2, text1, part)
    keep, term = call(
        keep_kernel,
        [shape(2 * SHARD, D, BF), packed],
        [SMEM] + [VMEM] * 4 + [anywhere],
        flops,
        scratch,
    )(grp, turned, raw_grad2, image_unit2, far, part)
    halves = (keep.astype(F32) + move(send, CORES).astype(F32)).astype(BF)
    mine = exchange(halves.reshape(8, SUB, D), FIRST)
    tiles = call(pack_kernel, [shape(768, 128, BF)], [VMEM], ROWS)(mine)[0]
    tiles, term = lax.optimization_barrier((tiles, term))
    tiles = tiles.reshape(16, 48, 128)
    term = shift(term, -1)
    done = total(exchange(tiles, FAR))
    done = (done.astype(F32) + move(done, swap_x((2, 2))).astype(F32)).astype(BF)
    done = spread(done, FAR).reshape(768, 128)[: 9 * BAND]
    done, term = lax.optimization_barrier((done, term))
    done = spread(done, NEAR)
    weight_grad = call(unpack_kernel, [shape(SHARD, D, F32)], [VMEM], ROWS)(done)[0]
    text_grad = call(finish_kernel, [shape(ROWS, D, F32)], [SMEM] * 2 + [VMEM] * 5, flops)(
        *numbers, image_unit2, image2, text0, grad, term
    )[0]
    return (weight_grad, text_grad)


def solution(mesh):
    return jax.shard_map(
        on_device,
        mesh=mesh,
        in_specs=(P(AXIS, None), P("grp", None), P(AXIS, None), P(AXIS), P(), P()),
        out_specs=(P("grp", None), P(AXIS, None)),
        check_vma=False,
    )
```

```python
import jax
import jax.numpy as jnp
from jax import lax
from jax.experimental import pallas as pl
from jax.experimental.pallas import tpu as pltpu
from jax.sharding import PartitionSpec as P

BF = jnp.bfloat16
F32 = jnp.float32
ROWS = 256
D = 1152
SHARD = D // 4
SUB = SHARD // 4
PACKED = ROWS + 16
BAND = SUB + 8
N = 512
AXIS = ("blk", "grp")
VMEM = pl.BlockSpec(memory_space=pltpu.VMEM)
SMEM = pl.BlockSpec(memory_space=pltpu.SMEM)


def coordinates(device):
    blk, grp = divmod(device, 4)
    return blk // 16, (blk // 8) % 2 * 2 + grp // 2, blk % 8, grp % 2


def device_at(z, x, y, core):
    return ((z % 8 * 2 + x % 4 // 2) * 8 + y % 8) * 4 + x % 2 * 2 + core


def swap_x(flips):
    moves = []
    for device in range(N):
        z, x, y, core = coordinates(device)
        moves.append((device_at(z, x ^ flips[core], y, core), device))
    return moves


def grouped(same, place):
    groups = {}
    for device in range(N):
        z, x, y, core = coordinates(device)
        key = (z + core) % 8, (x + core) % 4, (y + core) % 8, x % 2, core
        groups.setdefault(same(*key), []).append((place(*key), device))
    return [[device for _, device in sorted(group)] for group in groups.values()]


FIRST = grouped(lambda z, x, y, xl, core: (z // 2, x // 2, y // 2, core), lambda z, x, y, xl, core: (xl, z % 2, y % 2))
NEAR = grouped(lambda z, x, y, xl, core: (z // 2, x, y // 2, core), lambda z, x, y, xl, core: (z % 2, y % 2))
FAR = grouped(lambda z, x, y, xl, core: (z % 2, x, y % 2, core), lambda z, x, y, xl, core: (z // 2, y // 2))
CORES = [(i ^ 1, i) for i in range(N)]


def shift(block, distance):
    return lax.ppermute(block, AXIS, [((i - 4 * distance) % N, i) for i in range(N)])


def move(block, moves):
    return lax.ppermute(block, AXIS, moves)


def exchange(chunks, groups):
    return lax.all_to_all(chunks, AXIS, 0, 0, axis_index_groups=groups, tiled=True)


def spread(chunk, groups):
    return exchange(jnp.broadcast_to(chunk[None], (len(groups[0]),) + chunk.shape), groups)


def total(chunks):
    return jnp.sum(chunks.astype(F32), 0).astype(BF)


def call(kernel, outs, specs, flops, scratch=(), vmem=20):
    def run(*args):
        moved = sum(a.size * a.dtype.itemsize for a in args) + sum(
            o.size * o.dtype.itemsize for o in outs
        )
        return pl.pallas_call(
            kernel,
            out_shape=outs,
            in_specs=specs,
            out_specs=[VMEM] * len(outs),
            scratch_shapes=scratch,
            compiler_params=pltpu.CompilerParams(vmem_limit_bytes=vmem * 1024 * 1024),
            cost_estimate=pl.CostEstimate(flops=flops, bytes_accessed=moved if flops else 0, transcendentals=0),
        )(*args)

    return run


def top_row(ids_ref):
    first = lax.broadcasted_iota(jnp.int32, (16, ROWS), 0) == 0
    ids = jnp.broadcast_to(ids_ref[...].astype(F32), (16, ROWS))
    return jnp.where(first, ids, 0.0).astype(BF)


def put_ids(ids_ref, out_ref):
    out_ref[ROWS:, :ROWS] = top_row(ids_ref)
    out_ref[ROWS:, ROWS:] = jnp.zeros((16, D - ROWS), BF)


def prepare_kernel(feats_ref, text_ref, ids_ref, image_ref, out_ref, rows_ref, sems):
    loads = [
        pltpu.make_async_copy(text_ref, rows_ref, sems.at[0]),
        pltpu.make_async_copy(feats_ref, image_ref.at[pl.ds(0, ROWS), :], sems.at[1]),
    ]
    for load in loads:
        load.start()
    put_ids(ids_ref, image_ref)
    put_ids(ids_ref, out_ref)
    loads[0].wait()
    rows = rows_ref[...].astype(F32)
    inverse = 1.0 / jnp.sqrt(jnp.sum(rows * rows, -1, keepdims=True) + 1e-06)
    out_ref[:ROWS, :] = (rows * inverse).astype(BF)
    loads[1].wait()


def project(image_ref, weight_ref):
    raw = jnp.dot(image_ref[:ROWS, :], weight_ref[...], preferred_element_type=F32)
    inverse = 1.0 / jnp.sqrt(jnp.sum(raw * raw, -1, keepdims=True) + 1e-06)
    unit = raw * inverse
    return unit, unit.astype(BF), inverse


def ids_down(packed_ref):
    return across(packed_ref[ROWS:, :ROWS], jnp.ones((16, ROWS), BF))


def turn(image_ref):
    return image_ref[:ROWS, :].astype(F32).T.astype(BF)


def pair(image_unit, ids, text_ref, scale, bias):
    logits = (
        scale
        * lax.dot_general(
            image_unit, text_ref[:ROWS, :], (((1,), (1,)), ((), ())), preferred_element_type=F32
        )
        + bias
    )
    match = ids == text_ref[ROWS:, :ROWS].astype(F32)[0:1, :]
    weight = 1.0 / (1.0 + jnp.exp(jnp.where(match, logits, -logits)))
    return jnp.where(match, -weight, weight).astype(BF)


def across(left, right):
    return lax.dot_general(left, right, (((0,), (0,)), ((), ())), preferred_element_type=F32)


def back(image_grad, unit, inverse):
    inner = jnp.sum(image_grad * unit, -1, keepdims=True)
    return ((image_grad - unit * inner) * inverse).astype(BF)


def own_kernel(
    grp_ref, scale_ref, bias_ref, shard0_ref, shard1_ref, shard2_ref, shard3_ref, image_ref, text_ref, weight_ref, raw_grad_ref, grad_ref, sems
):
    grp = grp_ref[0]
    loads = []
    for flip, shard_ref in enumerate((shard0_ref, shard1_ref, shard2_ref, shard3_ref)):
        rows = pl.ds(pl.multiple_of((grp ^ flip) * SHARD, 32), SHARD)
        loads.append(pltpu.make_async_copy(shard_ref, weight_ref.at[rows, :], sems.at[flip]))
        loads[-1].start()
    for load in loads:
        load.wait()
    scale, bias = scale_ref[0], bias_ref[0]
    unit, image_unit, inverse = project(image_ref, weight_ref)
    near = pair(image_unit, ids_down(image_ref), text_ref, scale, bias)
    grad_ref[...] = across(near, image_unit)
    image_grad = scale * jnp.dot(near, text_ref[:ROWS, :], preferred_element_type=F32)
    raw_grad_ref[...] = back(image_grad, unit, inverse)


def next_kernel(
    scale_ref, bias_ref, weight_ref, image0_ref, raw_grad0_ref, image1_ref, text_ref, text1_ref, grad0_ref, part_ref, grad_ref,
    turned_ref, raw_grads_ref
):
    turned_ref[:, :ROWS] = turn(image0_ref)
    turned_ref[:, ROWS:] = turn(image1_ref)
    raw_grads_ref[:ROWS, :] = raw_grad0_ref[...]
    scale, bias = scale_ref[0], bias_ref[0]
    unit, image_unit, inverse = project(image1_ref, weight_ref)
    ids = ids_down(image1_ref)
    near = pair(image_unit, ids, text_ref, scale, bias)
    far = pair(image_unit, ids, text1_ref, scale, bias)
    grad_ref[...] = grad0_ref[...] + across(near, image_unit)
    image_grad = scale * (
        jnp.dot(near, text_ref[:ROWS, :], preferred_element_type=F32)
        + jnp.dot(far, text1_ref[:ROWS, :], preferred_element_type=F32)
    )
    raw_grads_ref[ROWS:, :] = back(image_grad, unit, inverse)
    part_ref[...] = jnp.dot(turned_ref[...], raw_grads_ref[...], preferred_element_type=F32)


def load_quarters(core, part_ref, rows_ref, sems):
    loads = []
    for half in range(2):
        at = pl.multiple_of((2 * half + core) * SHARD, 32)
        loads.append(
            pltpu.make_async_copy(
                part_ref.at[pl.ds(at, SHARD), :],
                rows_ref.at[pl.ds(half * SHARD, SHARD), :],
                sems.at[half],
            )
        )
    for load in loads:
        load.start()
    return loads


def add_quarters(core, turned_ref, raw_grad, rows_ref, loads, out_ref):
    for half in range(2):
        at = pl.multiple_of((2 * half + core) * SHARD, 32)
        rows = pl.ds(half * SHARD, SHARD)
        term = jnp.dot(turned_ref[pl.ds(at, SHARD), :], raw_grad, preferred_element_type=F32)
        loads[half].wait()
        out_ref[rows, :] = (rows_ref[rows, :] + term).astype(BF)


def last_kernel(
    grp_ref, scale_ref, bias_ref, weight_ref, image_ref, text1_ref, part_ref,
    send_ref, turned_ref, raw_grad_ref, image_unit_ref, far_ref, rows_ref, sems
):
    core = 1 - grp_ref[0] % 2
    loads = load_quarters(core, part_ref, rows_ref, sems)
    scale, bias = scale_ref[0], bias_ref[0]
    turned_ref[...] = turn(image_ref)
    unit, image_unit, inverse = project(image_ref, weight_ref)
    image_unit_ref[...] = image_unit
    far = pair(image_unit, ids_down(image_ref), text1_ref, scale, bias)
    far_ref[...] = far
    image_grad = scale * jnp.dot(far, text1_ref[:ROWS, :], preferred_element_type=F32)
    raw_grad = back(image_grad, unit, inverse)
    raw_grad_ref[...] = raw_grad
    add_quarters(core, turned_ref, raw_grad, rows_ref, loads, send_ref)


def keep_kernel(grp_ref, turned_ref, raw_grad_ref, image_unit_ref, far_ref, part_ref, keep_ref, back_ref, rows_ref, sems):
    core = grp_ref[0] % 2
    loads = load_quarters(core, part_ref, rows_ref, sems)
    add_quarters(core, turned_ref, raw_grad_ref[...], rows_ref, loads, keep_ref)
    back_ref[...] = across(far_ref[...], image_unit_ref[...]).astype(BF)


def finish_kernel(scale_ref, bias_ref, image_unit2_ref, image2_ref, text_ref, grad_ref, back_ref, out_ref):
    image_unit2 = image_unit2_ref[...]
    near2 = pair(image_unit2, ids_down(image2_ref), text_ref, scale_ref[0], bias_ref[0])
    out_ref[...] = scale_ref[0] * (grad_ref[...] + across(near2, image_unit2) + back_ref[...].astype(F32))


def pack_kernel(chunks_ref, out_ref):
    rows = chunks_ref[0].astype(F32)
    for chunk in range(1, 8):
        rows = rows + chunks_ref[chunk].astype(F32)
    for band in range(9):
        tile = jnp.concatenate([rows[:, band * 128 : (band + 1) * 128], jnp.zeros((8, 128), F32)], 0)
        out_ref[band * BAND : (band + 1) * BAND, :] = tile.astype(BF)
    out_ref[9 * BAND :, :] = jnp.zeros((768 - 9 * BAND, 128), BF)


def unpack_kernel(tiles_ref, out_ref):
    for chunk in range(4):
        for band in range(9):
            tile = tiles_ref[chunk, band * BAND : (band + 1) * BAND, :].astype(F32)
            out_ref[chunk * SUB : (chunk + 1) * SUB, band * 128 : (band + 1) * 128] = tile[:SUB]


def shape(rows, columns, dtype):
    return jax.ShapeDtypeStruct((rows, columns), dtype)


def on_device(feats, proj_weight, text_embed, row_ids, logit_scale, logit_bias):
    packed = shape(PACKED, D, BF)
    grp = lax.axis_index("grp").astype(jnp.int32).reshape(1)
    numbers = (logit_scale, logit_bias)
    flops = 2 * ROWS * D * D
    anywhere = pl.BlockSpec(memory_space=pl.ANY)
    hbm = pl.BlockSpec(memory_space=pltpu.HBM)
    scratch = [pltpu.VMEM((2 * SHARD, D), F32), pltpu.SemaphoreType.DMA((2,))]
    ids = row_ids.reshape(1, ROWS)
    image0, text0 = call(
        prepare_kernel,
        [packed] * 2,
        [hbm] * 2 + [VMEM],
        ROWS,
        [pltpu.VMEM((ROWS, D), BF), pltpu.SemaphoreType.DMA((2,))],
        62,
    )(feats, text_embed, ids)
    image1 = shift(image0, -1)
    text1 = shift(text0, 1)
    shard2 = move(proj_weight, swap_x((1, 3)))
    shard1 = move(proj_weight, CORES)
    shard3 = move(lax.optimization_barrier((shard2, text1, image1))[0], CORES)
    image2 = shift(image1, -1)
    weight, raw_grad0, grad = call(
        own_kernel, [shape(D, D, BF), shape(ROWS, D, BF), shape(ROWS, D, F32)], [SMEM] * 3 + [hbm] * 4 + [VMEM] * 2, 0,
        [pltpu.SemaphoreType.DMA((4,))],
    )(grp, *numbers, proj_weight, shard1, shard2, shard3, image0, text0)
    part, grad = call(
        next_kernel,
        [shape(D, D, F32), shape(ROWS, D, F32)],
        [SMEM] * 2 + [VMEM] * 7,
        0,
        [pltpu.VMEM((D, 2 * ROWS), BF), pltpu.VMEM((2 * ROWS, D), BF)],
    )(*numbers, weight, image0, raw_grad0, image1, text0, text1, grad)
    send, turned, raw_grad2, image_unit2, far = call(
        last_kernel,
        [shape(2 * SHARD, D, BF), shape(D, ROWS, BF), shape(ROWS, D, BF), shape(ROWS, D, BF), shape(ROWS, ROWS, BF)],
        [SMEM] * 3 + [VMEM] * 3 + [anywhere],
        2 * flops,
        scratch,
    )(grp, *numbers, weight, image2, text1, part)
    keep, term = call(
        keep_kernel,
        [shape(2 * SHARD, D, BF), shape(ROWS, D, BF)],
        [SMEM] + [VMEM] * 4 + [anywhere],
        flops,
        scratch,
    )(grp, turned, raw_grad2, image_unit2, far, part)
    halves = (keep.astype(F32) + move(send, CORES).astype(F32)).astype(BF)
    mine = exchange(halves.reshape(8, SUB, D), FIRST)
    tiles = call(pack_kernel, [shape(768, 128, BF)], [VMEM], ROWS)(mine)[0]
    tiles, term = lax.optimization_barrier((tiles, term))
    tiles = tiles.reshape(16, 48, 128)
    term = shift(term, -1)
    done = total(exchange(tiles, FAR))
    done = (done.astype(F32) + move(done, swap_x((2, 2))).astype(F32)).astype(BF)
    done = spread(done, FAR).reshape(768, 128)[: 9 * BAND]
    done, term = lax.optimization_barrier((done, term))
    done = spread(done, NEAR)
    weight_grad = call(unpack_kernel, [shape(SHARD, D, F32)], [VMEM], ROWS)(done)[0]
    text_grad = call(finish_kernel, [shape(ROWS, D, F32)], [SMEM] * 2 + [VMEM] * 5, flops)(
        *numbers, image_unit2, image2, text0, grad, term
    )[0]
    return (weight_grad, text_grad)


def solution(mesh):
    return jax.shard_map(
        on_device,
        mesh=mesh,
        in_specs=(P(AXIS, None), P("grp", None), P(AXIS, None), P(AXIS), P(), P()),
        out_specs=(P("grp", None), P(AXIS, None)),
        check_vma=False,
    )
```
